32 devices in a mesh: seq: 8 (over y, x, core), rep: 4 (over z).
Axes of the slice: x: 2, y: 2, z: 4, core: 2. Of those that a mesh axis runs over, the one named last changes fastest.
Arguments:
- tokens: bfloat16 [4, 1024, 1024], P('rep', 'seq'), may hold values from -16 to 16
- cotangent: bfloat16 [4, 1024, 1024], P('rep', 'seq'), may hold values from -6 to 6
- weights: bfloat16 [4, 1024, 512], replicated, may hold values from -0.1875 to 0.1875
- neighbour_lists: int32 [4, 8, 27], P('rep'), may hold values from 0 to 7, as said below
- neighbour_counts: int32 [4, 8], P('rep'), may hold values from 1 to 8, as said below
Outputs:
- output: bfloat16 [4, 1024, 1024], P('rep', 'seq')
- d_inputs: bfloat16 [4, 1024, 1024], P('rep', 'seq')
- weight_grads: float32 [4, 1024, 512], P(None, ('seq', 'rep'))
The draws below stay inside these ranges and needn't reach their ends.
Inputs may be any that keep to these rules, and one draw needn't show every extreme that they name: `neighbour_lists`: slot 0 of every list is the block itself; the live slots of a list name distinct blocks of the same replica's slab; dead slots hold the block's own position. `neighbour_counts`: in each replica some block has min(27, 8) live slots.
All inputs are finite; a program needn't handle non-finite values.
Results may differ from the reference program's by a relative error of at most 0.023.
The reference program's roundings to bfloat16 on the way count: a program that leaves them out, or rounds other values in their place, can miss the bound.
Values may be sent and summed in bfloat16 or wider, within the bound.
A program may use at most 128 MiB of HBM per device.

```python
import math
import jax
import jax.numpy as jnp
from jax import lax

D = 1024
HEADS = 8
HEAD_DIM = 64
BLOCK = 128
MAXN = 27
HD = 512
BLOCKS = 8
TOKENS = 1024
N_REP = 4


def neighbour_tables(key):
    key = jax.random.fold_in(key, 11)
    key_rank, key_count, key_pick = jax.random.split(key, 3)
    capacity = min(MAXN, BLOCKS)
    raw_bits = jax.random.randint(key_rank, (N_REP, BLOCKS, BLOCKS), 0, 1 << 20)
    block_ids = jnp.arange(BLOCKS, dtype=jnp.int32)
    ranked = raw_bits * BLOCKS + block_ids[None, None, :]
    ranked = jnp.where(block_ids[None, :, None] == block_ids[None, None, :], -1, ranked)
    ranking = jnp.argsort(ranked, axis=-1, stable=True).astype(jnp.int32)
    own_ids = jnp.broadcast_to(block_ids[None, :, None], (N_REP, BLOCKS, MAXN)).astype(jnp.int32)
    picked = jnp.concatenate([ranking[:, :, :capacity], own_ids[:, :, capacity:]], axis=-1)
    counts = jax.random.randint(key_count, (N_REP, BLOCKS), 1, capacity + 1)
    chosen = jax.random.randint(key_pick, (N_REP, 1), 0, BLOCKS)
    counts = jnp.where(block_ids[None, :] == chosen, capacity, counts).astype(jnp.int32)
    slot_ids = jnp.arange(MAXN, dtype=jnp.int32)
    lists = jnp.where(slot_ids[None, None, :] < counts[:, :, None], picked, own_ids).astype(jnp.int32)
    return (lists, counts)


def draw_neighbour_lists(key, part):
    return neighbour_tables(key)[0]


def draw_neighbour_counts(key, part):
    return neighbour_tables(key)[1]


def draw_tokens(key, part):
    dims_all = (N_REP, TOKENS, D)
    key_base = jax.random.fold_in(key, 0)
    return jnp.clip(jax.random.normal(key_base, dims_all, jnp.float32), -4.0, 4.0).astype(jnp.bfloat16)


def strengthened(array, own_key, source, target, parts, factor):
    def block_of(position):
        return (jnp.arange(array.shape[position]) // (array.shape[position] // parts)).reshape((-1,) + (1,) * (array.ndim - 1 - position))

    first = jax.random.permutation(own_key, parts)[block_of(target)]
    second = (block_of(target) + parts // 2) % parts
    return jnp.where((block_of(source) == first) | (block_of(source) == second), factor * array, array)


def steps_of(own_key, dims, cuts, low, largest):
    loudness, own = 1.0, jax.random.fold_in(own_key, 6)
    for dim, parts in cuts:
        heights = jnp.exp(jax.random.uniform(jax.random.fold_in(own, dim), (parts,), jnp.float32, low / len(cuts), largest / len(cuts)))
        loudness = loudness * jnp.repeat(heights, dims[dim] // parts).reshape([-1 if axis == dim else 1 for axis in range(len(dims))])
    return loudness


def centred(rng, shape, width, bound, shards=(), held_as=jnp.bfloat16):
    result = width * jax.random.normal(rng, shape, jnp.float32)
    if shards:
        result = result * steps_of(rng, shape, shards, -0.22, 0.18)
    return jnp.clip(result, -bound, bound).astype(held_as)


def bell_draw_with(key, dims, scale, limit, cuts, heavy, held_as=jnp.bfloat16):
    result = scale * jax.random.normal(key, dims, jnp.float32)
    if cuts:
        result = result * steps_of(key, dims, cuts, -0.22, 0.18)
    return jnp.clip(strengthened(result, jax.random.fold_in(key, 3), *heavy), -limit, limit).astype(held_as)


def setup_inputs(seed: int = 0) -> dict:
    splits = jax.random.split(jax.random.key(seed), 6)
    return {
        "tokens": draw_tokens(jax.random.fold_in(splits[5], 71), 0),
        "cotangent": bell_draw_with(splits[1], (N_REP, TOKENS, D), 1.0, 6.0, ((0, 4), (1, 8)), (1, 2, 8, 2.0)),
        "weights": centred(splits[2], (4, D, HD), D ** -0.5, 0.1875),
        "neighbour_lists": draw_neighbour_lists(jax.random.fold_in(splits[5], 71), 0),
        "neighbour_counts": draw_neighbour_counts(jax.random.fold_in(splits[5], 71), 0),
    }


def scores_of(query_block, slot_keys, live_count):
    score_scale = 1.0 / math.sqrt(HEAD_DIM)
    raw_scores = jnp.einsum('qhd,khd->hqk', query_block.astype(jnp.float32), slot_keys.astype(jnp.float32)) * score_scale
    live_cols = jnp.arange(slot_keys.shape[0]) // BLOCK < live_count
    return jnp.where(live_cols[None, None, :], raw_scores, -1e+30)

def one_replica(inputs, upstream, weights, lists, counts):
    score_scale = 1.0 / math.sqrt(HEAD_DIM)
    w_query, w_key, w_value, w_out = (weights[0], weights[1], weights[2], weights[3])
    shape_heads = (BLOCKS, BLOCK, HEADS, HEAD_DIM)
    queries = jnp.dot(inputs, w_query, preferred_element_type=jnp.float32).astype(jnp.bfloat16).reshape(shape_heads)
    key_rows = jnp.dot(inputs, w_key, preferred_element_type=jnp.float32).astype(jnp.bfloat16).reshape(shape_heads)
    value_rows = jnp.dot(inputs, w_value, preferred_element_type=jnp.float32).astype(jnp.bfloat16).reshape(shape_heads)

    def forward_block(block_data):
        query_block, slot_list, live_count = block_data
        slot_keys = key_rows[slot_list].reshape(MAXN * BLOCK, HEADS, HEAD_DIM)
        slot_values = value_rows[slot_list].reshape(MAXN * BLOCK, HEADS, HEAD_DIM)
        scores = scores_of(query_block, slot_keys, live_count)
        row_max = lax.optimization_barrier(jnp.max(scores, axis=-1))
        exponent = jnp.exp(scores - row_max[..., None])
        totals = lax.optimization_barrier(jnp.sum(exponent, axis=-1))
        mixed = jnp.einsum('hqk,khd->qhd', exponent.astype(jnp.bfloat16).astype(jnp.float32), slot_values.astype(jnp.float32))
        attended = (mixed / jnp.transpose(totals)[:, :, None]).astype(jnp.bfloat16)
        return (attended, row_max, totals)
    attended, row_max, totals = lax.map(forward_block, (queries, lists, counts))
    attended_flat = attended.reshape(TOKENS, HD)
    output = lax.dot_general(attended_flat, w_out, (((1,), (1,)), ((), ())), preferred_element_type=jnp.float32).astype(jnp.bfloat16)
    d_attended = jnp.dot(upstream, w_out, preferred_element_type=jnp.float32).astype(jnp.bfloat16)
    grad_out = lax.dot_general(upstream, attended_flat, (((0,), (0,)), ((), ())), preferred_element_type=jnp.float32)
    d_heads = d_attended.reshape(shape_heads)
    row_delta = lax.optimization_barrier(jnp.sum(d_heads.astype(jnp.float32) * attended.astype(jnp.float32), axis=-1))

    def backward_block(carry, block_data):
        key_acc, value_acc = carry
        query_block, d_block, delta_block, max_block, total_block, slot_list, live_count = block_data
        slot_keys = key_rows[slot_list].reshape(MAXN * BLOCK, HEADS, HEAD_DIM)
        slot_values = value_rows[slot_list].reshape(MAXN * BLOCK, HEADS, HEAD_DIM)
        scores = scores_of(query_block, slot_keys, live_count)
        normed = jnp.exp(scores - max_block[..., None]) / total_block[..., None]
        d_probs = jnp.einsum('qhd,khd->hqk', d_block.astype(jnp.float32), slot_values.astype(jnp.float32))
        d_scores = (normed * (d_probs - jnp.transpose(delta_block)[:, :, None])).astype(jnp.bfloat16)
        d_query = (jnp.einsum('hqk,khd->qhd', d_scores.astype(jnp.float32), slot_keys.astype(jnp.float32)) * score_scale).astype(jnp.bfloat16)
        key_terms = jnp.einsum('hqk,qhd->khd', d_scores.astype(jnp.float32), query_block.astype(jnp.float32)) * score_scale
        value_terms = jnp.einsum('hqk,qhd->khd', normed.astype(jnp.bfloat16).astype(jnp.float32), d_block.astype(jnp.float32))
        key_acc = key_acc.at[slot_list].add(key_terms.reshape(MAXN, BLOCK, HEADS, HEAD_DIM))
        value_acc = value_acc.at[slot_list].add(value_terms.reshape(MAXN, BLOCK, HEADS, HEAD_DIM))
        return ((key_acc, value_acc), d_query)
    zeros_acc = jnp.zeros(shape_heads, jnp.float32)
    (key_sum, value_sum), d_queries = lax.scan(backward_block, (zeros_acc, zeros_acc), (queries, d_heads, row_delta, row_max, totals, lists, counts))
    stacked = jnp.concatenate([d_queries.reshape(TOKENS, HD), key_sum.astype(jnp.bfloat16).reshape(TOKENS, HD), value_sum.astype(jnp.bfloat16).reshape(TOKENS, HD)], axis=1)
    w_joined = jnp.concatenate([w_query, w_key, w_value], axis=1)
    d_inputs = lax.dot_general(stacked, w_joined, (((1,), (1,)), ((), ())), preferred_element_type=jnp.float32).astype(jnp.bfloat16)
    grad_joined = lax.dot_general(inputs, stacked, (((0,), (0,)), ((), ())), preferred_element_type=jnp.float32)
    grad_three = jnp.transpose(grad_joined.reshape(D, 3, HD), (1, 0, 2))
    grads = jnp.concatenate([grad_three, grad_out[None]], axis=0)
    return (output, d_inputs, grads)

def reference(tokens, cotangent, weights, neighbour_lists, neighbour_counts):
    outputs_all = []
    inputs_grad_all = []
    grad_total = jnp.zeros((4, D, HD), jnp.float32)
    for replica in range(N_REP):
        output, d_inputs, grads = one_replica(tokens[replica], cotangent[replica], weights, neighbour_lists[replica], neighbour_counts[replica])
        outputs_all.append(output)
        inputs_grad_all.append(d_inputs)
        grad_total = grad_total + grads
    return (jnp.stack(outputs_all), jnp.stack(inputs_grad_all), grad_total)
```

```python
import functools
import math

import jax
import jax.numpy as jnp
from jax import lax
from jax.experimental import pallas as pl
from jax.experimental.pallas import tpu as pltpu
from jax.sharding import PartitionSpec as P

HEADS = 8
HEAD_DIM = 64
BLOCK = 128
MAXN = 27


F32 = jnp.float32
BF16 = jnp.bfloat16


def mm(a, b):
    return jnp.dot(a, b, preferred_element_type=F32)


def mm_nt(a, b):
    return lax.dot_general(a, b, (((1,), (1,)), ((), ())), preferred_element_type=F32)


def layer_kernel(
    n, reps,
    tok, cot, w, lists, counts,
    out, dinp, grads,
    send1, recv1, tstage, trecv, kt, vt, qtr, dtr, kx, vx, dkt, dvt, bias, xp, back, gs, gr,
    ss1, rs1, sst, rst, ssb, rsb, ssp, rsp, ssg, rsg,
):
    me = lax.axis_index("seq")
    rep = lax.axis_index("rep")
    core = lax.rem(me, 2)
    chip = me // 2
    chips = n // 2
    scale = 1.0 / math.sqrt(HEAD_DIM)
    hd = HEAD_DIM
    part = gs.shape[2]

    def remote(src, dst, s_sem, r_sem, seq, z):
        return pltpu.make_async_remote_copy(
            src_ref=src, dst_ref=dst, send_sem=s_sem, recv_sem=r_sem,
            device_id={"seq": seq, "rep": z}, device_id_type=pl.DeviceIdType.MESH,
        )

    barrier = pltpu.get_barrier_semaphore()

    def greet_seq(i, carry):
        pl.semaphore_signal(
            barrier, inc=1, device_id={"seq": lax.rem(me + i, n), "rep": rep},
            device_id_type=pl.DeviceIdType.MESH,
        )
        return carry

    def greet_rep(i, carry):
        pl.semaphore_signal(
            barrier, inc=1,
            device_id={
                "seq": lax.rem(me + 2 * lax.rem(i, chips), n),
                "rep": lax.rem(rep + 1 + i // chips, reps),
            },
            device_id_type=pl.DeviceIdType.MESH,
        )
        return carry

    lax.fori_loop(1, n, greet_seq, 0)
    lax.fori_loop(0, (reps - 1) * chips, greet_rep, 0)

    x = tok[0]
    g = cot[0]
    q = (mm(x, w[0]).astype(BF16).astype(F32) * scale).astype(BF16)
    k = mm(x, w[1]).astype(BF16)
    v = mm(x, w[2]).astype(BF16)
    da = mm(g, w[3]).astype(BF16)
    for h in range(n):
        cols = slice(h * hd, (h + 1) * hd)
        send1[h, 0] = jnp.concatenate([q[:, cols], k[:, cols]], axis=1)
        send1[h, 1] = jnp.concatenate([v[:, cols], da[:, cols]], axis=1)

    pl.semaphore_wait(barrier, n - 1 + (reps - 1) * chips)

    def heads_out(i):
        to = lax.rem(me + i, n)
        return remote(send1.at[to], recv1.at[me], ss1.at[to], rs1.at[me], to, rep)

    def heads_in(i):
        src = lax.rem(me + n - i, n)
        return remote(send1.at[src], recv1.at[src], ss1.at[src], rs1.at[src], src, rep)

    def start_heads(i, carry):
        heads_out(i).start()
        return carry

    lax.fori_loop(1, n, start_heads, 0)
    recv1[pl.ds(me, 1)] = send1[pl.ds(me, 1)]

    for s in range(n):
        rows = slice((s // 2) * BLOCK, (s // 2 + 1) * BLOCK)
        cols = slice(s * BLOCK, (s + 1) * BLOCK)
        tstage[s % 2, 0, rows] = tok[0, :, cols].T
        tstage[s % 2, 1, rows] = cot[0, :, cols].T

    def cols_out(i):
        to = lax.rem(me + i, n)
        return remote(
            tstage.at[lax.rem(to, 2)], trecv.at[me], sst.at[to], rst.at[me], to, rep
        )

    def cols_in(i):
        src = lax.rem(me + n - i, n)
        return remote(tstage.at[core], trecv.at[src], sst.at[src], rst.at[src], src, rep)

    def start_cols(i, carry):
        cols_out(i).start()
        return carry

    lax.fori_loop(1, n, start_cols, 0)
    trecv[pl.ds(me, 1)] = tstage[pl.ds(core, 1)]

    eye = lax.broadcasted_iota(jnp.int32, (n, n), 0) == lax.broadcasted_iota(jnp.int32, (n, n), 1)
    count_col = jnp.sum(
        jnp.where(eye, jnp.broadcast_to(counts[...].astype(F32), (n, n)), 0.0),
        axis=1, keepdims=True,
    )
    listed = lists[0]
    slot = lax.broadcasted_iota(jnp.int32, listed.shape, 1).astype(F32)
    alive = slot < count_col
    for c in range(n):
        hit = jnp.max(
            jnp.where(jnp.logical_and(listed == c, alive), 1.0, 0.0), axis=1, keepdims=True
        )
        bias[:, c * BLOCK : (c + 1) * BLOCK] = jnp.broadcast_to((hit - 1.0) * 1e30, (n, BLOCK))

    def wait_heads(i, carry):
        heads_in(i).wait_recv()
        return carry

    lax.fori_loop(1, n, wait_heads, 0)

    for b in range(n):
        rows = slice(b * BLOCK, (b + 1) * BLOCK)
        qk = recv1[b, 0]
        vd = recv1[b, 1]
        kx[rows] = qk[:, hd:]
        vx[rows] = vd[:, :hd]
        qkt = qk.T
        vdt = vd.T
        qtr[b] = qkt[:hd]
        kt[:, rows] = qkt[hd:]
        vt[:, rows] = vdt[:hd]
        dtr[b] = vdt[hd:]
    dkt[...] = jnp.zeros_like(dkt)
    dvt[...] = jnp.zeros_like(dvt)

    def back_out(b, piece):
        rows = pl.ds(pl.multiple_of(b * BLOCK, BLOCK), BLOCK)
        return remote(
            xp.at[core, piece, rows], back.at[me, piece],
            ssb.at[piece, b], rsb.at[piece, me], b, rep,
        )

    def back_in(h, piece):
        return remote(
            xp.at[core, piece, pl.ds(0, BLOCK)], back.at[h, piece],
            ssb.at[piece, h], rsb.at[piece, h], h, rep,
        )

    def attend(i, carry):
        b = lax.rem(me + 1 + i, n)
        rows = pl.ds(pl.multiple_of(b * BLOCK, BLOCK), BLOCK)
        qb = recv1[b, 0][:, :hd]
        dab = recv1[b, 1][:, hd:]
        s = mm(qb, kt[...]) + bias[pl.ds(b, 1), :]
        e = jnp.exp(s - jnp.max(s, axis=1, keepdims=True))
        total = jnp.sum(e, axis=1, keepdims=True)
        att = (mm(e.astype(BF16), vx[...]) / total).astype(BF16)
        delta = jnp.sum(dab.astype(F32) * att.astype(F32), axis=1, keepdims=True)
        normed = e * (1.0 / total)
        ds = (normed * (mm(dab, vt[...]) - delta)).astype(BF16)
        dq = (mm(ds, kx[...]) * scale).astype(BF16)
        dkt[...] += mm(qtr[b], ds)
        dvt[...] += mm(dtr[b], normed.astype(BF16))
        xp[core, 0, rows] = jnp.concatenate([att, dq], axis=1)

        @pl.when(b != me)
        def _():
            back_out(b, 0).start()

        return carry

    lax.fori_loop(0, n, attend, 0)

    other = me + 1 - 2 * core

    def pair_out(piece):
        return remote(
            xp.at[core, piece], xp.at[core, piece], ssp.at[piece], rsp.at[piece], other, rep
        )

    def pair_in(piece):
        return remote(
            xp.at[1 - core, piece], xp.at[1 - core, piece],
            ssp.at[piece], rsp.at[piece], other, rep,
        )

    pair_out(0).start()
    for b in range(n):
        rows = slice(b * BLOCK, (b + 1) * BLOCK)
        both = jnp.concatenate([dkt[:, rows], dvt[:, rows]], axis=0)
        xp[core, 1, rows] = both.T.astype(BF16)
    pair_out(1).start()

    def start_back(i, carry):
        back_out(lax.rem(me + i, n), 1).start()
        return carry

    lax.fori_loop(1, n, start_back, 0)
    mine = pl.ds(pl.multiple_of(me * BLOCK, BLOCK), BLOCK)
    for piece in range(2):
        back[me, piece] = xp[core, piece, mine]

    def wait_cols(i, carry):
        cols_in(i).wait_recv()
        return carry

    lax.fori_loop(1, n, wait_cols, 0)
    t_all = jnp.concatenate([trecv[b, 0] for b in range(n)], axis=1)
    c_all = jnp.concatenate([trecv[b, 1] for b in range(n)], axis=1)
    pair_in(0).wait_recv()
    gq = mm(t_all, jnp.concatenate([xp[0, 0][:, hd:], xp[1, 0][:, hd:]], axis=1))
    go = mm(c_all, jnp.concatenate([xp[0, 0][:, :hd], xp[1, 0][:, :hd]], axis=1))
    gs[:, 0] = gq.astype(BF16).reshape(chips * reps, part, 2 * hd)
    gs[:, 3] = go.astype(BF16).reshape(chips * reps, part, 2 * hd)
    pair_in(1).wait_recv()
    gk = mm(t_all, jnp.concatenate([xp[0, 1][:, :hd], xp[1, 1][:, :hd]], axis=1))
    gv = mm(t_all, jnp.concatenate([xp[0, 1][:, hd:], xp[1, 1][:, hd:]], axis=1))
    gs[:, 1] = gk.astype(BF16).reshape(chips * reps, part, 2 * hd)
    gs[:, 2] = gv.astype(BF16).reshape(chips * reps, part, 2 * hd)

    def grads_out(i):
        chip_to = lax.rem(chip + i, chips)
        rep_to = lax.rem(rep + i // chips, reps)
        to = chip_to * reps + rep_to
        return remote(
            gs.at[to], gr.at[chip * reps + rep], ssg.at[to], rsg.at[chip * reps + rep],
            2 * chip_to + core, rep_to,
        )

    def grads_in(i):
        chip_from = lax.rem(chip + i, chips)
        rep_from = lax.rem(rep + i // chips, reps)
        src = chip_from * reps + rep_from
        return remote(
            gs.at[src], gr.at[src], ssg.at[src], rsg.at[src], 2 * chip_from + core, rep_from
        )

    def start_grads(i, carry):
        grads_out(i).start()
        return carry

    lax.fori_loop(1, chips * reps, start_grads, 0)
    gr[pl.ds(chip * reps + rep, 1)] = gs[pl.ds(chip * reps + rep, 1)]

    def wait_back(i, carry):
        src = lax.rem(me + n - i, n)
        back_in(src, 0).wait_recv()
        back_in(src, 1).wait_recv()
        return carry

    lax.fori_loop(1, n, wait_back, 0)
    att = jnp.concatenate([back[h, 0][:, :hd] for h in range(n)], axis=1)
    dq = jnp.concatenate([back[h, 0][:, hd:] for h in range(n)], axis=1)
    dk = jnp.concatenate([back[h, 1][:, :hd] for h in range(n)], axis=1)
    dv = jnp.concatenate([back[h, 1][:, hd:] for h in range(n)], axis=1)
    out[0] = mm_nt(att, w[3]).astype(BF16)
    dinp[0] = (mm_nt(dq, w[0]) + mm_nt(dk, w[1]) + mm_nt(dv, w[2])).astype(BF16)

    def wait_grads(i, carry):
        grads_in(i).wait_recv()
        return carry

    lax.fori_loop(1, chips * reps, wait_grads, 0)
    for c in range(chips):
        acc = gr[c * reps].astype(F32)
        for r in range(1, reps):
            acc = acc + gr[c * reps + r].astype(F32)
        grads[:, :, c * 2 * hd : (c + 1) * 2 * hd] = acc

    def drain(i, carry):
        heads_out(i).wait_send()
        cols_out(i).wait_send()
        back_out(lax.rem(me + i, n), 0).wait_send()
        back_out(lax.rem(me + i, n), 1).wait_send()
        return carry

    lax.fori_loop(1, n, drain, 0)
    pair_out(0).wait_send()
    pair_out(1).wait_send()

    def drain_grads(i, carry):
        grads_out(i).wait_send()
        return carry

    lax.fori_loop(1, chips * reps, drain_grads, 0)


def by_heads(n, reps, tokens, cotangent, weights, neighbour_lists, neighbour_counts):
    width = tokens.shape[2]
    slab = n * BLOCK
    cols = weights.shape[2]
    part = width // (n * reps)
    groups = (n // 2) * reps
    vmem = pl.BlockSpec(memory_space=pltpu.VMEM)
    dma = pltpu.SemaphoreType.DMA
    return pl.pallas_call(
        functools.partial(layer_kernel, n, reps),
        out_shape=(
            jax.ShapeDtypeStruct(tokens.shape, BF16),
            jax.ShapeDtypeStruct(tokens.shape, BF16),
            jax.ShapeDtypeStruct((4, part, cols), F32),
        ),
        in_specs=[vmem] * 5,
        out_specs=(vmem, vmem, vmem),
        scratch_shapes=[
            pltpu.VMEM((n, 2, BLOCK, 2 * HEAD_DIM), BF16),
            pltpu.VMEM((n, 2, BLOCK, 2 * HEAD_DIM), BF16),
            pltpu.VMEM((2, 2, width // 2, BLOCK), BF16),
            pltpu.VMEM((n, 2, width // 2, BLOCK), BF16),
            pltpu.VMEM((HEAD_DIM, slab), BF16),
            pltpu.VMEM((HEAD_DIM, slab), BF16),
            pltpu.VMEM((n, HEAD_DIM, BLOCK), BF16),
            pltpu.VMEM((n, HEAD_DIM, BLOCK), BF16),
            pltpu.VMEM((slab, HEAD_DIM), BF16),
            pltpu.VMEM((slab, HEAD_DIM), BF16),
            pltpu.VMEM((HEAD_DIM, slab), F32),
            pltpu.VMEM((HEAD_DIM, slab), F32),
            pltpu.VMEM((n, slab), F32),
            pltpu.VMEM((2, 2, slab, 2 * HEAD_DIM), BF16),
            pltpu.VMEM((n, 2, BLOCK, 2 * HEAD_DIM), BF16),
            pltpu.VMEM((groups, 4, part, 2 * HEAD_DIM), BF16),
            pltpu.VMEM((groups, 4, part, 2 * HEAD_DIM), BF16),
            dma((n,)), dma((n,)), dma((n,)), dma((n,)),
            dma((2, n)), dma((2, n)), dma((2,)), dma((2,)),
            dma((groups,)), dma((groups,)),
        ],
        compiler_params=pltpu.CompilerParams(
            collective_id=0, has_side_effects=True, vmem_limit_bytes=48 * 1024 * 1024
        ),
        cost_estimate=pl.CostEstimate(
            flops=3 * 10**9, bytes_accessed=6 * 2**20, transcendentals=2**20
        ),
    )(tokens, cotangent, weights, neighbour_lists, neighbour_counts)


def split_heads(matrix):
    return matrix.reshape(matrix.shape[:-1] + (HEADS, HEAD_DIM))


def body(tokens, cotangent, weights, neighbour_lists, neighbour_counts):
    score_scale = 1.0 / math.sqrt(HEAD_DIM)
    inputs = tokens[0]
    upstream = cotangent[0]
    row_count = inputs.shape[0]
    local_blocks = row_count // BLOCK
    w_query, w_key, w_value, w_out = (weights[0], weights[1], weights[2], weights[3])
    queries = (
        jnp.dot(inputs, w_query, preferred_element_type=jnp.float32)
        .astype(jnp.bfloat16)
        .reshape(local_blocks, BLOCK, -1)
    )
    key_rows = (
        jnp.dot(inputs, w_key, preferred_element_type=jnp.float32)
        .astype(jnp.bfloat16)
        .reshape(local_blocks, BLOCK, -1)
    )
    value_rows = (
        jnp.dot(inputs, w_value, preferred_element_type=jnp.float32)
        .astype(jnp.bfloat16)
        .reshape(local_blocks, BLOCK, -1)
    )
    all_keys, all_values = (
        lax.all_gather(key_rows, "seq", axis=0, tiled=True),
        lax.all_gather(value_rows, "seq", axis=0, tiled=True),
    )
    slab_blocks = all_keys.shape[0]
    first_block = lax.axis_index("seq") * local_blocks
    lists_all = neighbour_lists[0]
    counts_all = neighbour_counts[0]
    my_lists = lax.dynamic_slice_in_dim(lists_all, first_block, local_blocks, 0)
    my_counts = lax.dynamic_slice_in_dim(counts_all, first_block, local_blocks, 0)
    slot_keys = split_heads(
        jnp.take(all_keys, my_lists, axis=0).reshape(local_blocks, MAXN * BLOCK, -1)
    )
    slot_values = split_heads(
        jnp.take(all_values, my_lists, axis=0).reshape(local_blocks, MAXN * BLOCK, -1)
    )
    query_heads = split_heads(queries)
    scores = (
        jnp.einsum("bqhd,bkhd->bhqk", query_heads, slot_keys, preferred_element_type=jnp.float32)
        * score_scale
    )
    live_cols = (jnp.arange(MAXN * BLOCK) // BLOCK)[None, :] < my_counts[:, None]
    scores = jnp.where(live_cols[:, None, None, :], scores, -1e30)
    row_max = jnp.max(scores, axis=-1)
    exponent = jnp.exp(scores - row_max[..., None])
    totals = jnp.sum(exponent, axis=-1)
    mixed = jnp.einsum(
        "bhqk,bkhd->bqhd",
        exponent.astype(jnp.bfloat16),
        slot_values,
        preferred_element_type=jnp.float32,
    )
    attended = (
        (mixed / jnp.transpose(totals, (0, 2, 1))[..., None])
        .astype(jnp.bfloat16)
        .reshape(row_count, -1)
    )
    output = lax.dot_general(
        attended, w_out, (((1,), (1,)), ((), ())), preferred_element_type=jnp.float32
    ).astype(jnp.bfloat16)
    d_attended = jnp.dot(upstream, w_out, preferred_element_type=jnp.float32).astype(jnp.bfloat16)
    grad_out = lax.dot_general(
        upstream, attended, (((0,), (0,)), ((), ())), preferred_element_type=jnp.float32
    )
    d_blocks = d_attended.reshape(local_blocks, BLOCK, -1)
    d_heads = split_heads(d_blocks)
    attended_heads = split_heads(attended.reshape(local_blocks, BLOCK, -1))
    row_delta = jnp.transpose(
        jnp.sum(d_heads.astype(jnp.float32) * attended_heads.astype(jnp.float32), axis=-1),
        (0, 2, 1),
    )
    normed = exponent / totals[..., None]
    d_probs = jnp.einsum(
        "bqhd,bkhd->bhqk", d_heads, slot_values, preferred_element_type=jnp.float32
    )
    d_scores = (normed * (d_probs - row_delta[..., None])).astype(jnp.bfloat16)
    d_queries = (
        (
            jnp.einsum("bhqk,bkhd->bqhd", d_scores, slot_keys, preferred_element_type=jnp.float32)
            * score_scale
        )
        .astype(jnp.bfloat16)
        .reshape(row_count, -1)
    )
    gathered_query, gathered_dattn = (
        lax.all_gather(queries, "seq", axis=0, tiled=True),
        lax.all_gather(d_blocks, "seq", axis=0, tiled=True),
    )
    gathered_max, gathered_total, gathered_delta = (
        lax.all_gather(row_max, "seq", axis=0, tiled=True),
        lax.all_gather(totals, "seq", axis=0, tiled=True),
        lax.all_gather(row_delta, "seq", axis=0, tiled=True),
    )
    owners = first_block + jnp.arange(local_blocks)
    live_slots = jnp.arange(MAXN)[None, :] < counts_all[:, None]
    listed = jnp.any(
        (lists_all[:, :, None] == owners[None, None, :]) & live_slots[:, :, None], axis=1
    )
    groups = slab_blocks // 8
    own_keys = split_heads(key_rows)
    own_values = split_heads(value_rows)

    def regroup(matrix):
        return matrix.reshape((groups, 8) + matrix.shape[1:])

    def accumulate(carry, group_data):
        group_query, group_dattn, group_max, group_total, group_delta, group_listed = group_data
        group_query = split_heads(group_query)
        group_dattn = split_heads(group_dattn)
        group_scores = (
            jnp.einsum(
                "cqhd,ikhd->cihqk", group_query, own_keys, preferred_element_type=jnp.float32
            )
            * score_scale
        )
        group_scores = jnp.where(group_listed[:, :, None, None, None], group_scores, -1e30)
        group_probs = (
            jnp.exp(group_scores - group_max[:, None, :, :, None])
            / group_total[:, None, :, :, None]
        )
        group_dprobs = jnp.einsum(
            "cqhd,ikhd->cihqk", group_dattn, own_values, preferred_element_type=jnp.float32
        )
        group_dscores = (group_probs * (group_dprobs - group_delta[:, None, :, :, None])).astype(
            jnp.bfloat16
        )
        key_next = carry[0] + jnp.einsum(
            "cihqk,cqhd->ikhd", group_dscores, group_query, preferred_element_type=jnp.float32
        )
        value_next = carry[1] + jnp.einsum(
            "cihqk,cqhd->ikhd",
            group_probs.astype(jnp.bfloat16),
            group_dattn,
            preferred_element_type=jnp.float32,
        )
        return ((key_next, value_next), None)

    zero_sum = jnp.zeros((local_blocks, BLOCK, HEADS, HEAD_DIM), jnp.float32)
    group_inputs = (
        regroup(gathered_query),
        regroup(gathered_dattn),
        regroup(gathered_max),
        regroup(gathered_total),
        regroup(gathered_delta),
        regroup(listed),
    )
    (key_heads, value_heads), _ = lax.scan(accumulate, (zero_sum, zero_sum), group_inputs)
    key_sum = (key_heads * score_scale).reshape(local_blocks, BLOCK, -1)
    value_sum = value_heads.reshape(local_blocks, BLOCK, -1)
    d_keys = key_sum.astype(jnp.bfloat16).reshape(row_count, -1)
    d_values = value_sum.astype(jnp.bfloat16).reshape(row_count, -1)
    stacked = jnp.concatenate([d_queries, d_keys, d_values], axis=1)
    w_joined = jnp.concatenate([w_query, w_key, w_value], axis=1)
    d_inputs = lax.dot_general(
        stacked, w_joined, (((1,), (1,)), ((), ())), preferred_element_type=jnp.float32
    ).astype(jnp.bfloat16)
    grad_joined = lax.dot_general(
        inputs, stacked, (((0,), (0,)), ((), ())), preferred_element_type=jnp.float32
    )
    width_model = inputs.shape[1]
    grad_three = jnp.transpose(grad_joined.reshape(width_model, 3, -1), (1, 0, 2))
    grads = jnp.concatenate([grad_three, grad_out[None]], axis=0)
    within_slab = lax.psum_scatter(
        grads.astype(jnp.bfloat16), "seq", scatter_dimension=1, tiled=True
    )
    summed = lax.psum_scatter(within_slab, "rep", scatter_dimension=1, tiled=True).astype(
        jnp.float32
    )
    return (output[None], d_inputs[None], summed)


def solution(mesh):
    placed = (
        P("rep", "seq", None),
        P("rep", "seq", None),
        P(),
        P("rep", None, None),
        P("rep", None),
    )
    n, reps = mesh.shape["seq"], mesh.shape["rep"]
    run = functools.partial(by_heads, n, reps) if n == HEADS else body
    return jax.shard_map(
        run,
        mesh=mesh,
        in_specs=placed,
        out_specs=(P("rep", "seq", None), P("rep", "seq", None), P(None, ("seq", "rep"), None)),
        check_vma=False,
    )
```

```python
import functools
import math

import jax
import jax.numpy as jnp
from jax import lax
from jax.experimental import pallas as pl
from jax.experimental.pallas import tpu as pltpu
from jax.sharding import PartitionSpec as P

HEADS = 8
HEAD_DIM = 64
BLOCK = 128
MAXN = 27


F32 = jnp.float32
BF16 = jnp.bfloat16


def mm(a, b):
    return jnp.dot(a, b, preferred_element_type=F32)


def mm_nt(a, b):
    return lax.dot_general(a, b, (((1,), (1,)), ((), ())), preferred_element_type=F32)


def layer_kernel(
    n, reps,
    tok_hbm, cot_hbm, w_hbm, lists, counts,
    out, dinp, grads,
    tok, cot, w, send1, recv1, tstage, trecv, kt, vt, qtr, dtr, kx, vx, dkt, dvt, bias,
    normed_all, att_all, xp, back, gs, gr,
    ls, ss1, rs1, sst, rst, ssb, rsb, ssp, rsp, ssg, rsg,
):
    me = lax.axis_index("seq")
    rep = lax.axis_index("rep")
    core = lax.rem(me, 2)
    chip = me // 2
    chips = n // 2
    scale = 1.0 / math.sqrt(HEAD_DIM)
    hd = HEAD_DIM
    part = gs.shape[2]

    loads = [
        pltpu.make_async_copy(cot_hbm.at[0], cot, ls.at[0]),
        pltpu.make_async_copy(tok_hbm.at[0], tok, ls.at[1]),
    ] + [pltpu.make_async_copy(w_hbm.at[j], w.at[j], ls.at[2 + j]) for j in range(4)]
    for load in loads:
        load.start()

    def remote(src, dst, s_sem, r_sem, seq, z):
        return pltpu.make_async_remote_copy(
            src_ref=src, dst_ref=dst, send_sem=s_sem, recv_sem=r_sem,
            device_id={"seq": seq, "rep": z}, device_id_type=pl.DeviceIdType.MESH,
        )

    barrier = pltpu.get_barrier_semaphore()

    def greet_seq(i, carry):
        pl.semaphore_signal(
            barrier, inc=1, device_id={"seq": lax.rem(me + i, n), "rep": rep},
            device_id_type=pl.DeviceIdType.MESH,
        )
        return carry

    def greet_rep(i, carry):
        pl.semaphore_signal(
            barrier, inc=1,
            device_id={
                "seq": lax.rem(me + 2 * lax.rem(i, chips), n),
                "rep": lax.rem(rep + 1 + i // chips, reps),
            },
            device_id_type=pl.DeviceIdType.MESH,
        )
        return carry

    lax.fori_loop(1, n, greet_seq, 0)
    lax.fori_loop(0, (reps - 1) * chips, greet_rep, 0)

    def each_peer(act):
        def step(i, carry):
            act(lax.rem(me + i, n))
            return carry

        lax.fori_loop(1, n, step, 0)

    def stage_cols(kind, ref):
        for s in range(n):
            rows = slice((s // 2) * BLOCK, (s // 2 + 1) * BLOCK)
            tstage[s % 2, kind, rows] = ref[:, s * BLOCK : (s + 1) * BLOCK].T

    def cols_out(to, kind):
        return remote(
            tstage.at[lax.rem(to, 2), kind], trecv.at[me, kind],
            sst.at[kind, to], rst.at[kind, me], to, rep,
        )

    def cols_in(src, kind):
        return remote(
            tstage.at[core, kind], trecv.at[src, kind],
            sst.at[kind, src], rst.at[kind, src], src, rep,
        )

    loads[0].wait()
    stage_cols(1, cot)
    pl.semaphore_wait(barrier, n - 1 + (reps - 1) * chips)
    far = 2 * (chips - 1 - chip)
    cols_out(far, 1).start()
    cols_out(far + 1, 1).start()
    loads[1].wait()

    def heads_out(to, piece):
        return remote(
            send1.at[to, piece], recv1.at[me, piece],
            ss1.at[piece, to], rs1.at[piece, me], to, rep,
        )

    def heads_in(src, piece):
        return remote(
            send1.at[src, piece], recv1.at[src, piece],
            ss1.at[piece, src], rs1.at[piece, src], src, rep,
        )

    def pack(piece, one, two):
        for h in range(n):
            cols = slice(h * hd, (h + 1) * hd)
            send1[h, piece] = jnp.concatenate([one[:, cols], two[:, cols]], axis=1)
        each_peer(lambda to: heads_out(to, piece).start())
        recv1[me, piece] = send1[me, piece]

    x = tok[...]
    loads[2].wait()
    q = (mm(x, w[0]).astype(BF16).astype(F32) * scale).astype(BF16)
    loads[3].wait()
    k = mm(x, w[1]).astype(BF16)
    pack(0, q, k)
    loads[4].wait()
    v = mm(x, w[2]).astype(BF16)
    loads[5].wait()
    da = mm(cot[...], w[3]).astype(BF16)
    pack(1, v, da)

    def rest_cols(to):
        @pl.when(to // 2 != chips - 1 - chip)
        def _():
            cols_out(to, 1).start()

    each_peer(rest_cols)
    stage_cols(0, tok)
    each_peer(lambda to: cols_out(to, 0).start())
    trecv[pl.ds(me, 1)] = tstage[pl.ds(core, 1)]

    eye = lax.broadcasted_iota(jnp.int32, (n, n), 0) == lax.broadcasted_iota(jnp.int32, (n, n), 1)
    count_col = jnp.sum(
        jnp.where(eye, jnp.broadcast_to(counts[...].astype(F32), (n, n)), 0.0),
        axis=1, keepdims=True,
    )
    listed = lists[0]
    slot = lax.broadcasted_iota(jnp.int32, listed.shape, 1).astype(F32)
    alive = slot < count_col
    for c in range(n):
        hit = jnp.max(
            jnp.where(jnp.logical_and(listed == c, alive), 1.0, 0.0), axis=1, keepdims=True
        )
        bias[:, c * BLOCK : (c + 1) * BLOCK] = jnp.broadcast_to((hit - 1.0) * 1e30, (n, BLOCK))
    dkt[...] = jnp.zeros_like(dkt)
    dvt[...] = jnp.zeros_like(dvt)

    each_peer(lambda src: heads_in(src, 0).wait_recv())
    for b in range(n):
        rows = slice(b * BLOCK, (b + 1) * BLOCK)
        qk = recv1[b, 0]
        kx[rows] = qk[:, hd:]
        qkt = qk.T
        qtr[b] = qkt[:hd]
        kt[:, rows] = qkt[hd:]
    each_peer(lambda src: heads_in(src, 1).wait_recv())
    for b in range(n):
        rows = slice(b * BLOCK, (b + 1) * BLOCK)
        vd = recv1[b, 1]
        vx[rows] = vd[:, :hd]
        vdt = vd.T
        vt[:, rows] = vdt[:hd]
        dtr[b] = vdt[hd:]

    def back_out(b, piece):
        rows = pl.ds(pl.multiple_of(b * BLOCK, BLOCK), BLOCK)
        return remote(
            xp.at[core, piece, rows], back.at[me, piece],
            ssb.at[piece, b], rsb.at[piece, me], b, rep,
        )

    def back_in(h, piece):
        return remote(
            xp.at[core, piece, pl.ds(0, BLOCK)], back.at[h, piece],
            ssb.at[piece, h], rsb.at[piece, h], h, rep,
        )

    other = me + 1 - 2 * core

    def pair_out(piece):
        return remote(
            xp.at[core, piece], xp.at[core, piece], ssp.at[piece], rsp.at[piece], other, rep
        )

    def pair_in(piece):
        return remote(
            xp.at[1 - core, piece], xp.at[1 - core, piece],
            ssp.at[piece], rsp.at[piece], other, rep,
        )

    def forward(b, carry):
        rows = pl.ds(pl.multiple_of(b * BLOCK, BLOCK), BLOCK)
        s = mm(recv1[b, 0][:, :hd], kt[...]) + bias[pl.ds(b, 1), :]
        e = jnp.exp(s - jnp.max(s, axis=1, keepdims=True))
        total = jnp.sum(e, axis=1, keepdims=True)
        att_all[rows] = (mm(e.astype(BF16), vx[...]) / total).astype(BF16)
        normed = e * (1.0 / total)
        normed_all[b] = normed
        dvt[...] += mm(dtr[b], normed.astype(BF16))
        return carry

    lax.fori_loop(0, n, forward, 0)

    for b in range(n):
        rows = slice(b * BLOCK, (b + 1) * BLOCK)
        xp[core, 0, rows] = jnp.concatenate([att_all[rows], dvt[:, rows].T.astype(BF16)], axis=1)
    pair_out(0).start()
    each_peer(lambda to: back_out(to, 0).start())

    def backward(b, carry):
        rows = pl.ds(pl.multiple_of(b * BLOCK, BLOCK), BLOCK)
        dab = recv1[b, 1][:, hd:]
        delta = jnp.sum(dab.astype(F32) * att_all[rows].astype(F32), axis=1, keepdims=True)
        ds = (normed_all[b] * (mm(dab, vt[...]) - delta)).astype(BF16)
        dkt[...] += mm(qtr[b], ds)
        xp[core, 1, rows] = jnp.concatenate(
            [(mm(ds, kx[...]) * scale).astype(BF16), jnp.zeros((BLOCK, hd), BF16)], axis=1
        )
        return carry

    def grads_out(i, k0, count, stage):
        chip_to = lax.rem(chip + i, chips)
        rep_to = lax.rem(rep + i // chips, reps)
        to = chip_to * reps + rep_to
        here = chip * reps + rep
        return remote(
            gs.at[to, pl.ds(k0, count)], gr.at[here, pl.ds(k0, count)],
            ssg.at[stage, to], rsg.at[stage, here], 2 * chip_to + core, rep_to,
        )

    def grads_in(i, k0, count, stage):
        chip_from = lax.rem(chip + i, chips)
        rep_from = lax.rem(rep + i // chips, reps)
        src = chip_from * reps + rep_from
        return remote(
            gs.at[src, pl.ds(k0, count)], gr.at[src, pl.ds(k0, count)],
            ssg.at[stage, src], rsg.at[stage, src], 2 * chip_from + core, rep_from,
        )

    stages = ((3, 1, 0), (2, 1, 1), (0, 2, 2))

    def each_group(act):
        def step(i, carry):
            act(i)
            return carry

        lax.fori_loop(1, chips * reps, step, 0)

    def product(kind, left, piece, cols):
        right = jnp.concatenate([xp[0, piece][:, cols], xp[1, piece][:, cols]], axis=1)
        gs[:, kind] = mm(left, right).astype(BF16).reshape(chips * reps, part, 2 * hd)

    low, high = slice(0, hd), slice(hd, 2 * hd)
    lax.fori_loop(0, n // 2, backward, 0)
    each_peer(lambda src: cols_in(src, 1).wait_recv())
    pair_in(0).wait_recv()
    product(3, jnp.concatenate([trecv[b, 1] for b in range(n)], axis=1), 0, low)
    each_group(lambda i: grads_out(i, *stages[0]).start())
    lax.fori_loop(n // 2, n, backward, 0)

    for b in range(n):
        rows = slice(b * BLOCK, (b + 1) * BLOCK)
        xp[core, 1, rows] = jnp.concatenate(
            [xp[core, 1, rows][:, :hd], dkt[:, rows].T.astype(BF16)], axis=1
        )
    pair_out(1).start()
    each_peer(lambda to: back_out(to, 1).start())
    mine = pl.ds(pl.multiple_of(me * BLOCK, BLOCK), BLOCK)
    for piece in range(2):
        back[me, piece] = xp[core, piece, mine]

    each_peer(lambda src: cols_in(src, 0).wait_recv())
    t_all = jnp.concatenate([trecv[b, 0] for b in range(n)], axis=1)
    product(2, t_all, 0, high)
    each_group(lambda i: grads_out(i, *stages[1]).start())
    pair_in(1).wait_recv()
    product(0, t_all, 1, low)
    product(1, t_all, 1, high)
    each_group(lambda i: grads_out(i, *stages[2]).start())
    gr[pl.ds(chip * reps + rep, 1)] = gs[pl.ds(chip * reps + rep, 1)]

    each_peer(lambda src: back_in(src, 0).wait_recv())
    att = jnp.concatenate([back[h, 0][:, :hd] for h in range(n)], axis=1)
    dv = jnp.concatenate([back[h, 0][:, hd:] for h in range(n)], axis=1)
    out[0] = mm_nt(att, w[3]).astype(BF16)
    each_peer(lambda src: back_in(src, 1).wait_recv())
    dq = jnp.concatenate([back[h, 1][:, :hd] for h in range(n)], axis=1)
    dk = jnp.concatenate([back[h, 1][:, hd:] for h in range(n)], axis=1)
    dinp[0] = (mm_nt(dq, w[0]) + mm_nt(dk, w[1]) + mm_nt(dv, w[2])).astype(BF16)

    for stage in stages:
        each_group(lambda i, stage=stage: grads_in(i, *stage).wait_recv())
    for c in range(chips):
        acc = gr[c * reps].astype(F32)
        for r in range(1, reps):
            acc = acc + gr[c * reps + r].astype(F32)
        grads[:, :, c * 2 * hd : (c + 1) * 2 * hd] = acc

    def drain(to):
        for piece in range(2):
            heads_out(to, piece).wait_send()
            cols_out(to, piece).wait_send()
            back_out(to, piece).wait_send()

    each_peer(drain)
    pair_out(0).wait_send()
    pair_out(1).wait_send()
    for stage in stages:
        each_group(lambda i, stage=stage: grads_out(i, *stage).wait_send())


def by_heads(n, reps, tokens, cotangent, weights, neighbour_lists, neighbour_counts):
    width = tokens.shape[2]
    slab = n * BLOCK
    cols = weights.shape[2]
    part = width // (n * reps)
    groups = (n // 2) * reps
    vmem = pl.BlockSpec(memory_space=pltpu.VMEM)
    hbm = pl.BlockSpec(memory_space=pl.ANY)
    dma = pltpu.SemaphoreType.DMA
    return pl.pallas_call(
        functools.partial(layer_kernel, n, reps),
        out_shape=(
            jax.ShapeDtypeStruct(tokens.shape, BF16),
            jax.ShapeDtypeStruct(tokens.shape, BF16),
            jax.ShapeDtypeStruct((4, part, cols), F32),
        ),
        in_specs=[hbm] * 3 + [vmem] * 2,
        out_specs=(vmem, vmem, vmem),
        scratch_shapes=[
            pltpu.VMEM((BLOCK, width), BF16),
            pltpu.VMEM((BLOCK, width), BF16),
            pltpu.VMEM(weights.shape, BF16),
            pltpu.VMEM((n, 2, BLOCK, 2 * HEAD_DIM), BF16),
            pltpu.VMEM((n, 2, BLOCK, 2 * HEAD_DIM), BF16),
            pltpu.VMEM((2, 2, width // 2, BLOCK), BF16),
            pltpu.VMEM((n, 2, width // 2, BLOCK), BF16),
            pltpu.VMEM((HEAD_DIM, slab), BF16),
            pltpu.VMEM((HEAD_DIM, slab), BF16),
            pltpu.VMEM((n, HEAD_DIM, BLOCK), BF16),
            pltpu.VMEM((n, HEAD_DIM, BLOCK), BF16),
            pltpu.VMEM((slab, HEAD_DIM), BF16),
            pltpu.VMEM((slab, HEAD_DIM), BF16),
            pltpu.VMEM((HEAD_DIM, slab), F32),
            pltpu.VMEM((HEAD_DIM, slab), F32),
            pltpu.VMEM((n, slab), F32),
            pltpu.VMEM((n, BLOCK, slab), F32),
            pltpu.VMEM((slab, HEAD_DIM), BF16),
            pltpu.VMEM((2, 2, slab, 2 * HEAD_DIM), BF16),
            pltpu.VMEM((n, 2, BLOCK, 2 * HEAD_DIM), BF16),
            pltpu.VMEM((groups, 4, part, 2 * HEAD_DIM), BF16),
            pltpu.VMEM((groups, 4, part, 2 * HEAD_DIM), BF16),
            dma((6,)),
            dma((2, n)), dma((2, n)), dma((2, n)), dma((2, n)), dma((2, n)), dma((2, n)),
            dma((2,)), dma((2,)), dma((3, groups)), dma((3, groups)),
        ],
        compiler_params=pltpu.CompilerParams(
            collective_id=0, has_side_effects=True, vmem_limit_bytes=56 * 1024 * 1024
        ),
        cost_estimate=pl.CostEstimate(
            flops=3 * 10**9, bytes_accessed=6 * 2**20, transcendentals=2**20
        ),
    )(tokens, cotangent, weights, neighbour_lists, neighbour_counts)


def split_heads(matrix):
    return matrix.reshape(matrix.shape[:-1] + (HEADS, HEAD_DIM))


def body(tokens, cotangent, weights, neighbour_lists, neighbour_counts):
    score_scale = 1.0 / math.sqrt(HEAD_DIM)
    inputs = tokens[0]
    upstream = cotangent[0]
    row_count = inputs.shape[0]
    local_blocks = row_count // BLOCK
    w_query, w_key, w_value, w_out = (weights[0], weights[1], weights[2], weights[3])
    queries = (
        jnp.dot(inputs, w_query, preferred_element_type=jnp.float32)
        .astype(jnp.bfloat16)
        .reshape(local_blocks, BLOCK, -1)
    )
    key_rows = (
        jnp.dot(inputs, w_key, preferred_element_type=jnp.float32)
        .astype(jnp.bfloat16)
        .reshape(local_blocks, BLOCK, -1)
    )
    value_rows = (
        jnp.dot(inputs, w_value, preferred_element_type=jnp.float32)
        .astype(jnp.bfloat16)
        .reshape(local_blocks, BLOCK, -1)
    )
    all_keys, all_values = (
        lax.all_gather(key_rows, "seq", axis=0, tiled=True),
        lax.all_gather(value_rows, "seq", axis=0, tiled=True),
    )
    slab_blocks = all_keys.shape[0]
    first_block = lax.axis_index("seq") * local_blocks
    lists_all = neighbour_lists[0]
    counts_all = neighbour_counts[0]
    my_lists = lax.dynamic_slice_in_dim(lists_all, first_block, local_blocks, 0)
    my_counts = lax.dynamic_slice_in_dim(counts_all, first_block, local_blocks, 0)
    slot_keys = split_heads(
        jnp.take(all_keys, my_lists, axis=0).reshape(local_blocks, MAXN * BLOCK, -1)
    )
    slot_values = split_heads(
        jnp.take(all_values, my_lists, axis=0).reshape(local_blocks, MAXN * BLOCK, -1)
    )
    query_heads = split_heads(queries)
    scores = (
        jnp.einsum("bqhd,bkhd->bhqk", query_heads, slot_keys, preferred_element_type=jnp.float32)
        * score_scale
    )
    live_cols = (jnp.arange(MAXN * BLOCK) // BLOCK)[None, :] < my_counts[:, None]
    scores = jnp.where(live_cols[:, None, None, :], scores, -1e30)
    row_max = jnp.max(scores, axis=-1)
    exponent = jnp.exp(scores - row_max[..., None])
    totals = jnp.sum(exponent, axis=-1)
    mixed = jnp.einsum(
        "bhqk,bkhd->bqhd",
        exponent.astype(jnp.bfloat16),
        slot_values,
        preferred_element_type=jnp.float32,
    )
    attended = (
        (mixed / jnp.transpose(totals, (0, 2, 1))[..., None])
        .astype(jnp.bfloat16)
        .reshape(row_count, -1)
    )
    output = lax.dot_general(
        attended, w_out, (((1,), (1,)), ((), ())), preferred_element_type=jnp.float32
    ).astype(jnp.bfloat16)
    d_attended = jnp.dot(upstream, w_out, preferred_element_type=jnp.float32).astype(jnp.bfloat16)
    grad_out = lax.dot_general(
        upstream, attended, (((0,), (0,)), ((), ())), preferred_element_type=jnp.float32
    )
    d_blocks = d_attended.reshape(local_blocks, BLOCK, -1)
    d_heads = split_heads(d_blocks)
    attended_heads = split_heads(attended.reshape(local_blocks, BLOCK, -1))
    row_delta = jnp.transpose(
        jnp.sum(d_heads.astype(jnp.float32) * attended_heads.astype(jnp.float32), axis=-1),
        (0, 2, 1),
    )
    normed = exponent / totals[..., None]
    d_probs = jnp.einsum(
        "bqhd,bkhd->bhqk", d_heads, slot_values, preferred_element_type=jnp.float32
    )
    d_scores = (normed * (d_probs - row_delta[..., None])).astype(jnp.bfloat16)
    d_queries = (
        (
            jnp.einsum("bhqk,bkhd->bqhd", d_scores, slot_keys, preferred_element_type=jnp.float32)
            * score_scale
        )
        .astype(jnp.bfloat16)
        .reshape(row_count, -1)
    )
    gathered_query, gathered_dattn = (
        lax.all_gather(queries, "seq", axis=0, tiled=True),
        lax.all_gather(d_blocks, "seq", axis=0, tiled=True),
    )
    gathered_max, gathered_total, gathered_delta = (
        lax.all_gather(row_max, "seq", axis=0, tiled=True),
        lax.all_gather(totals, "seq", axis=0, tiled=True),
        lax.all_gather(row_delta, "seq", axis=0, tiled=True),
    )
    owners = first_block + jnp.arange(local_blocks)
    live_slots = jnp.arange(MAXN)[None, :] < counts_all[:, None]
    listed = jnp.any(
        (lists_all[:, :, None] == owners[None, None, :]) & live_slots[:, :, None], axis=1
    )
    groups = slab_blocks // 8
    own_keys = split_heads(key_rows)
    own_values = split_heads(value_rows)

    def regroup(matrix):
        return matrix.reshape((groups, 8) + matrix.shape[1:])

    def accumulate(carry, group_data):
        group_query, group_dattn, group_max, group_total, group_delta, group_listed = group_data
        group_query = split_heads(group_query)
        group_dattn = split_heads(group_dattn)
        group_scores = (
            jnp.einsum(
                "cqhd,ikhd->cihqk", group_query, own_keys, preferred_element_type=jnp.float32
            )
            * score_scale
        )
        group_scores = jnp.where(group_listed[:, :, None, None, None], group_scores, -1e30)
        group_probs = (
            jnp.exp(group_scores - group_max[:, None, :, :, None])
            / group_total[:, None, :, :, None]
        )
        group_dprobs = jnp.einsum(
            "cqhd,ikhd->cihqk", group_dattn, own_values, preferred_element_type=jnp.float32
        )
        group_dscores = (group_probs * (group_dprobs - group_delta[:, None, :, :, None])).astype(
            jnp.bfloat16
        )
        key_next = carry[0] + jnp.einsum(
            "cihqk,cqhd->ikhd", group_dscores, group_query, preferred_element_type=jnp.float32
        )
        value_next = carry[1] + jnp.einsum(
            "cihqk,cqhd->ikhd",
            group_probs.astype(jnp.bfloat16),
            group_dattn,
            preferred_element_type=jnp.float32,
        )
        return ((key_next, value_next), None)

    zero_sum = jnp.zeros((local_blocks, BLOCK, HEADS, HEAD_DIM), jnp.float32)
    group_inputs = (
        regroup(gathered_query),
        regroup(gathered_dattn),
        regroup(gathered_max),
        regroup(gathered_total),
        regroup(gathered_delta),
        regroup(listed),
    )
    (key_heads, value_heads), _ = lax.scan(accumulate, (zero_sum, zero_sum), group_inputs)
    key_sum = (key_heads * score_scale).reshape(local_blocks, BLOCK, -1)
    value_sum = value_heads.reshape(local_blocks, BLOCK, -1)
    d_keys = key_sum.astype(jnp.bfloat16).reshape(row_count, -1)
    d_values = value_sum.astype(jnp.bfloat16).reshape(row_count, -1)
    stacked = jnp.concatenate([d_queries, d_keys, d_values], axis=1)
    w_joined = jnp.concatenate([w_query, w_key, w_value], axis=1)
    d_inputs = lax.dot_general(
        stacked, w_joined, (((1,), (1,)), ((), ())), preferred_element_type=jnp.float32
    ).astype(jnp.bfloat16)
    grad_joined = lax.dot_general(
        inputs, stacked, (((0,), (0,)), ((), ())), preferred_element_type=jnp.float32
    )
    width_model = inputs.shape[1]
    grad_three = jnp.transpose(grad_joined.reshape(width_model, 3, -1), (1, 0, 2))
    grads = jnp.concatenate([grad_three, grad_out[None]], axis=0)
    within_slab = lax.psum_scatter(
        grads.astype(jnp.bfloat16), "seq", scatter_dimension=1, tiled=True
    )
    summed = lax.psum_scatter(within_slab, "rep", scatter_dimension=1, tiled=True).astype(
        jnp.float32
    )
    return (output[None], d_inputs[None], summed)


def solution(mesh):
    placed = (
        P("rep", "seq", None),
        P("rep", "seq", None),
        P(),
        P("rep", None, None),
        P("rep", None),
    )
    n, reps = mesh.shape["seq"], mesh.shape["rep"]
    run = functools.partial(by_heads, n, reps) if n == HEADS else body
    return jax.shard_map(
        run,
        mesh=mesh,
        in_specs=placed,
        out_specs=(P("rep", "seq", None), P("rep", "seq", None), P(None, ("seq", "rep"), None)),
        check_vma=False,
    )
```

```python
import functools
import math

import jax
import jax.numpy as jnp
from jax import lax
from jax.experimental import pallas as pl
from jax.experimental.pallas import tpu as pltpu
from jax.sharding import PartitionSpec as P

HEADS = 8
HEAD_DIM = 64
BLOCK = 128
MAXN = 27


F32 = jnp.float32
BF16 = jnp.bfloat16


def mm(a, b):
    return jnp.dot(a, b, preferred_element_type=F32)


def mm_nt(a, b):
    return lax.dot_general(a, b, (((1,), (1,)), ((), ())), preferred_element_type=F32)


def layer_kernel(
    n, reps,
    tok_hbm, cot_hbm, w_hbm, lists, counts,
    out, dinp, grads,
    tok, cot, w, send1, recv1, tstage, trecv, kt, vt, qtr, dtr, kx, vx, dkt, dvt, bias,
    normed_all, att_all, dq_all, xp, bk, back, gs, gr,
    ls, ss1, rs1, sst, rst, srl, ssb, rsb, ssp, rsp, ssg, rsg,
):
    me = lax.axis_index("seq")
    rep = lax.axis_index("rep")
    core = lax.rem(me, 2)
    chip = me // 2
    chips = n // 2
    scale = 1.0 / math.sqrt(HEAD_DIM)
    hd = HEAD_DIM
    part = gs.shape[2]

    loads = [
        pltpu.make_async_copy(cot_hbm.at[0], cot, ls.at[0]),
        pltpu.make_async_copy(tok_hbm.at[0], tok, ls.at[1]),
    ] + [pltpu.make_async_copy(w_hbm.at[j], w.at[j], ls.at[2 + j]) for j in range(4)]
    for load in loads:
        load.start()

    def remote(src, dst, s_sem, r_sem, seq, z):
        return pltpu.make_async_remote_copy(
            src_ref=src, dst_ref=dst, send_sem=s_sem, recv_sem=r_sem,
            device_id={"seq": seq, "rep": z}, device_id_type=pl.DeviceIdType.MESH,
        )

    barrier = pltpu.get_barrier_semaphore()

    def greet_seq(i, carry):
        pl.semaphore_signal(
            barrier, inc=1, device_id={"seq": lax.rem(me + i, n), "rep": rep},
            device_id_type=pl.DeviceIdType.MESH,
        )
        return carry

    def greet_rep(i, carry):
        pl.semaphore_signal(
            barrier, inc=1,
            device_id={
                "seq": lax.rem(me + 2 * lax.rem(i, chips), n),
                "rep": lax.rem(rep + 1 + i // chips, reps),
            },
            device_id_type=pl.DeviceIdType.MESH,
        )
        return carry

    lax.fori_loop(1, n, greet_seq, 0)
    lax.fori_loop(0, (reps - 1) * chips, greet_rep, 0)

    def each_peer(act):
        def step(i, carry):
            act(lax.rem(me + i, n))
            return carry

        lax.fori_loop(1, n, step, 0)

    x_chip = chip + 1 - 2 * lax.rem(chip, 2)
    y_chip = chip + 2 - 4 * (chip // 2)
    far_chip = chips - 1 - chip
    other = me + 1 - 2 * core

    def stage_cols(kind, ref):
        for s in range(n):
            cols = slice((s // 2) * BLOCK, (s // 2 + 1) * BLOCK)
            tstage[s % 2, kind, :, cols] = ref[:, s * BLOCK : (s + 1) * BLOCK]

    def cols_out(to, kind):
        return remote(
            tstage.at[lax.rem(to, 2), kind], trecv.at[me, kind],
            sst.at[kind, to], rst.at[kind, me], to, rep,
        )

    def cols_in(src, kind):
        return remote(
            tstage.at[core, kind], trecv.at[src, kind],
            sst.at[kind, src], rst.at[kind, src], src, rep,
        )

    def cols_on(kind, k):
        src, to = (y_chip, x_chip) if kind == 0 else (x_chip, y_chip)
        block = 2 * src + k
        return remote(
            trecv.at[block, kind], trecv.at[block, kind],
            srl.at[kind, k], rst.at[kind, block], 2 * to + core, rep,
        )

    def near(kind, act):
        act(other, kind)
        for k in range(2):
            act(2 * x_chip + k, kind)
            act(2 * y_chip + k, kind)

    def forward_cols(kind):
        for k in range(2):
            cols_in(2 * (y_chip if kind == 0 else x_chip) + k, kind).wait_recv()
            cols_on(kind, k).start()

    def finish_cols(kind):
        cols_in(other, kind).wait_recv()
        for k in range(2):
            cols_in(2 * (x_chip if kind == 0 else y_chip) + k, kind).wait_recv()
            cols_in(2 * far_chip + k, kind).wait_recv()

    loads[0].wait()
    stage_cols(1, cot)
    pl.semaphore_wait(barrier, n - 1 + (reps - 1) * chips)
    near(1, lambda to, kind: cols_out(to, kind).start())
    loads[1].wait()
    stage_cols(0, tok)

    def heads_out(to, piece):
        return remote(
            send1.at[to, piece], recv1.at[me, piece],
            ss1.at[piece, to], rs1.at[piece, me], to, rep,
        )

    def heads_in(src, piece):
        return remote(
            send1.at[src, piece], recv1.at[src, piece],
            ss1.at[piece, src], rs1.at[piece, src], src, rep,
        )

    def pack(piece, one, two):
        for h in range(n):
            cols = slice(h * hd, (h + 1) * hd)
            send1[h, piece] = jnp.concatenate([one[:, cols], two[:, cols]], axis=1)
        each_peer(lambda to: heads_out(to, piece).start())
        recv1[me, piece] = send1[me, piece]

    x = tok[...]
    loads[2].wait()
    q = (mm(x, w[0]).astype(BF16).astype(F32) * scale).astype(BF16)
    loads[3].wait()
    k = mm(x, w[1]).astype(BF16)
    pack(0, q, k)
    loads[4].wait()
    v = mm(x, w[2]).astype(BF16)
    loads[5].wait()
    da = mm(cot[...], w[3]).astype(BF16)
    pack(1, v, da)

    near(0, lambda to, kind: cols_out(to, kind).start())
    trecv[pl.ds(me, 1)] = tstage[pl.ds(core, 1)]

    eye = lax.broadcasted_iota(jnp.int32, (n, n), 0) == lax.broadcasted_iota(jnp.int32, (n, n), 1)
    count_col = jnp.sum(
        jnp.where(eye, jnp.broadcast_to(counts[...].astype(F32), (n, n)), 0.0),
        axis=1, keepdims=True,
    )
    listed = lists[0]
    slot = lax.broadcasted_iota(jnp.int32, listed.shape, 1).astype(F32)
    alive = slot < count_col
    for c in range(n):
        hit = jnp.max(
            jnp.where(jnp.logical_and(listed == c, alive), 1.0, 0.0), axis=1, keepdims=True
        )
        bias[:, c * BLOCK : (c + 1) * BLOCK] = jnp.broadcast_to((hit - 1.0) * 1e30, (n, BLOCK))
    dkt[...] = jnp.zeros_like(dkt)
    dvt[...] = jnp.zeros_like(dvt)

    each_peer(lambda src: heads_in(src, 0).wait_recv())
    for b in range(n):
        rows = slice(b * BLOCK, (b + 1) * BLOCK)
        qk = recv1[b, 0]
        kx[rows] = qk[:, hd:]
        qkt = qk.T
        qtr[b] = qkt[:hd]
        kt[:, rows] = qkt[hd:]
    each_peer(lambda src: heads_in(src, 1).wait_recv())
    for b in range(n):
        rows = slice(b * BLOCK, (b + 1) * BLOCK)
        vd = recv1[b, 1]
        vx[rows] = vd[:, :hd]
        vdt = vd.T
        vt[:, rows] = vdt[:hd]
        dtr[b] = vdt[hd:]

    forward_cols(1)

    def back_out(b, piece):
        rows = pl.ds(pl.multiple_of(b * BLOCK, BLOCK), BLOCK)
        return remote(
            bk.at[piece, rows], back.at[me, piece],
            ssb.at[piece, b], rsb.at[piece, me], b, rep,
        )

    def back_in(h, piece):
        return remote(
            bk.at[piece, pl.ds(0, BLOCK)], back.at[h, piece],
            ssb.at[piece, h], rsb.at[piece, h], h, rep,
        )

    def pair_out(piece):
        return remote(
            xp.at[core, piece], xp.at[core, piece], ssp.at[piece], rsp.at[piece], other, rep
        )

    def pair_in(piece):
        return remote(
            xp.at[1 - core, piece], xp.at[1 - core, piece],
            ssp.at[piece], rsp.at[piece], other, rep,
        )

    def forward(b, carry):
        rows = pl.ds(pl.multiple_of(b * BLOCK, BLOCK), BLOCK)
        s = mm(recv1[b, 0][:, :hd], kt[...]) + bias[pl.ds(b, 1), :]
        e = jnp.exp(s - jnp.max(s, axis=1, keepdims=True))
        total = jnp.sum(e, axis=1, keepdims=True)
        att = (mm(e.astype(BF16), vx[...]) / total).astype(BF16)
        att_all[rows] = att
        xp[core, 0, :hd, rows] = att.T
        normed = e * (1.0 / total)
        normed_all[b] = normed
        dvt[...] += mm(dtr[b], normed.astype(BF16))
        return carry

    lax.fori_loop(0, n, forward, 0)
    xp[core, 0, hd:] = dvt[...].astype(BF16)
    pair_out(0).start()

    for b in range(n):
        rows = slice(b * BLOCK, (b + 1) * BLOCK)
        bk[0, rows] = jnp.concatenate([att_all[rows], dvt[:, rows].T.astype(BF16)], axis=1)
    each_peer(lambda to: back_out(to, 0).start())
    forward_cols(0)

    def backward(b, carry):
        rows = pl.ds(pl.multiple_of(b * BLOCK, BLOCK), BLOCK)
        dab = recv1[b, 1][:, hd:]
        delta = jnp.sum(dab.astype(F32) * att_all[rows].astype(F32), axis=1, keepdims=True)
        ds = (normed_all[b] * (mm(dab, vt[...]) - delta)).astype(BF16)
        dkt[...] += mm(qtr[b], ds)
        dq = (mm(ds, kx[...]) * scale).astype(BF16)
        dq_all[rows] = dq
        xp[core, 1, :hd, rows] = dq.T
        return carry

    def grads_out(i, k0, count, stage):
        chip_to = lax.rem(chip + i, chips)
        rep_to = lax.rem(rep + i // chips, reps)
        to = chip_to * reps + rep_to
        here = chip * reps + rep
        return remote(
            gs.at[to, pl.ds(k0, count)], gr.at[here, pl.ds(k0, count)],
            ssg.at[stage, to], rsg.at[stage, here], 2 * chip_to + core, rep_to,
        )

    def grads_in(i, k0, count, stage):
        chip_from = lax.rem(chip + i, chips)
        rep_from = lax.rem(rep + i // chips, reps)
        src = chip_from * reps + rep_from
        return remote(
            gs.at[src, pl.ds(k0, count)], gr.at[src, pl.ds(k0, count)],
            ssg.at[stage, src], rsg.at[stage, src], 2 * chip_from + core, rep_from,
        )

    stages = ((3, 1, 0), (2, 1, 1), (0, 2, 2))

    def each_group(act):
        def step(i, carry):
            act(i)
            return carry

        lax.fori_loop(1, chips * reps, step, 0)

    def product(kinds, column_kind, piece, rows):
        left = jnp.concatenate(
            [xp[c, piece][r] for r in rows for c in range(2)], axis=0
        )
        right = trecv[:, column_kind].reshape(n * BLOCK, trecv.shape[3])
        total = mm(left, right).astype(BF16)
        for j, kind in enumerate(kinds):
            one = total[2 * hd * j : 2 * hd * (j + 1)].T
            gs[:, kind] = one.reshape(chips * reps, part, 2 * hd)

    low, high = slice(0, hd), slice(hd, 2 * hd)
    lax.fori_loop(0, 2, backward, 0)
    finish_cols(1)
    pair_in(0).wait_recv()
    product((3,), 1, 0, (low,))
    each_group(lambda i: grads_out(i, *stages[0]).start())
    lax.fori_loop(2, n, backward, 0)

    xp[core, 1, hd:] = dkt[...].astype(BF16)
    pair_out(1).start()
    finish_cols(0)
    product((2,), 0, 0, (high,))
    each_group(lambda i: grads_out(i, *stages[1]).start())
    pair_in(1).wait_recv()
    product((0, 1), 0, 1, (low, high))
    each_group(lambda i: grads_out(i, *stages[2]).start())
    gr[pl.ds(chip * reps + rep, 1)] = gs[pl.ds(chip * reps + rep, 1)]

    for b in range(n):
        rows = slice(b * BLOCK, (b + 1) * BLOCK)
        bk[1, rows] = jnp.concatenate([dq_all[rows], dkt[:, rows].T.astype(BF16)], axis=1)
    each_peer(lambda to: back_out(to, 1).start())
    mine = pl.ds(pl.multiple_of(me * BLOCK, BLOCK), BLOCK)
    for piece in range(2):
        back[me, piece] = bk[piece, mine]

    each_peer(lambda src: back_in(src, 0).wait_recv())
    att = jnp.concatenate([back[h, 0][:, :hd] for h in range(n)], axis=1)
    dv = jnp.concatenate([back[h, 0][:, hd:] for h in range(n)], axis=1)
    out[0] = mm_nt(att, w[3]).astype(BF16)
    each_peer(lambda src: back_in(src, 1).wait_recv())
    dq = jnp.concatenate([back[h, 1][:, :hd] for h in range(n)], axis=1)
    dk = jnp.concatenate([back[h, 1][:, hd:] for h in range(n)], axis=1)
    dinp[0] = (mm_nt(dq, w[0]) + mm_nt(dk, w[1]) + mm_nt(dv, w[2])).astype(BF16)

    for stage in stages:
        each_group(lambda i, stage=stage: grads_in(i, *stage).wait_recv())
    for c in range(chips):
        acc = gr[c * reps].astype(F32)
        for r in range(1, reps):
            acc = acc + gr[c * reps + r].astype(F32)
        grads[:, :, c * 2 * hd : (c + 1) * 2 * hd] = acc

    def drain(to):
        for piece in range(2):
            heads_out(to, piece).wait_send()
            back_out(to, piece).wait_send()

    each_peer(drain)
    for kind in range(2):
        near(kind, lambda to, kind: cols_out(to, kind).wait_send())
        for k in range(2):
            cols_on(kind, k).wait_send()
    pair_out(0).wait_send()
    pair_out(1).wait_send()
    for stage in stages:
        each_group(lambda i, stage=stage: grads_out(i, *stage).wait_send())


def by_heads(n, reps, tokens, cotangent, weights, neighbour_lists, neighbour_counts):
    width = tokens.shape[2]
    slab = n * BLOCK
    cols = weights.shape[2]
    part = width // (n * reps)
    groups = (n // 2) * reps
    vmem = pl.BlockSpec(memory_space=pltpu.VMEM)
    hbm = pl.BlockSpec(memory_space=pl.ANY)
    dma = pltpu.SemaphoreType.DMA
    return pl.pallas_call(
        functools.partial(layer_kernel, n, reps),
        out_shape=(
            jax.ShapeDtypeStruct(tokens.shape, BF16),
            jax.ShapeDtypeStruct(tokens.shape, BF16),
            jax.ShapeDtypeStruct((4, part, cols), F32),
        ),
        in_specs=[hbm] * 3 + [vmem] * 2,
        out_specs=(vmem, vmem, vmem),
        scratch_shapes=[
            pltpu.VMEM((BLOCK, width), BF16),
            pltpu.VMEM((BLOCK, width), BF16),
            pltpu.VMEM(weights.shape, BF16),
            pltpu.VMEM((n, 2, BLOCK, 2 * HEAD_DIM), BF16),
            pltpu.VMEM((n, 2, BLOCK, 2 * HEAD_DIM), BF16),
            pltpu.VMEM((2, 2, BLOCK, width // 2), BF16),
            pltpu.VMEM((n, 2, BLOCK, width // 2), BF16),
            pltpu.VMEM((HEAD_DIM, slab), BF16),
            pltpu.VMEM((HEAD_DIM, slab), BF16),
            pltpu.VMEM((n, HEAD_DIM, BLOCK), BF16),
            pltpu.VMEM((n, HEAD_DIM, BLOCK), BF16),
            pltpu.VMEM((slab, HEAD_DIM), BF16),
            pltpu.VMEM((slab, HEAD_DIM), BF16),
            pltpu.VMEM((HEAD_DIM, slab), F32),
            pltpu.VMEM((HEAD_DIM, slab), F32),
            pltpu.VMEM((n, slab), F32),
            pltpu.VMEM((n, BLOCK, slab), F32),
            pltpu.VMEM((slab, HEAD_DIM), BF16),
            pltpu.VMEM((slab, HEAD_DIM), BF16),
            pltpu.VMEM((2, 2, 2 * HEAD_DIM, slab), BF16),
            pltpu.VMEM((2, slab, 2 * HEAD_DIM), BF16),
            pltpu.VMEM((n, 2, BLOCK, 2 * HEAD_DIM), BF16),
            pltpu.VMEM((groups, 4, part, 2 * HEAD_DIM), BF16),
            pltpu.VMEM((groups, 4, part, 2 * HEAD_DIM), BF16),
            dma((6,)),
            dma((2, n)), dma((2, n)), dma((2, n)), dma((2, n)), dma((2, 2)),
            dma((2, n)), dma((2, n)),
            dma((2,)), dma((2,)), dma((3, groups)), dma((3, groups)),
        ],
        compiler_params=pltpu.CompilerParams(
            collective_id=0, has_side_effects=True, vmem_limit_bytes=53 * 1024 * 1024
        ),
        cost_estimate=pl.CostEstimate(
            flops=3 * 10**9, bytes_accessed=6 * 2**20, transcendentals=2**20
        ),
    )(tokens, cotangent, weights, neighbour_lists, neighbour_counts)


def split_heads(matrix):
    return matrix.reshape(matrix.shape[:-1] + (HEADS, HEAD_DIM))


def body(tokens, cotangent, weights, neighbour_lists, neighbour_counts):
    score_scale = 1.0 / math.sqrt(HEAD_DIM)
    inputs = tokens[0]
    upstream = cotangent[0]
    row_count = inputs.shape[0]
    local_blocks = row_count // BLOCK
    w_query, w_key, w_value, w_out = (weights[0], weights[1], weights[2], weights[3])
    queries = (
        jnp.dot(inputs, w_query, preferred_element_type=jnp.float32)
        .astype(jnp.bfloat16)
        .reshape(local_blocks, BLOCK, -1)
    )
    key_rows = (
        jnp.dot(inputs, w_key, preferred_element_type=jnp.float32)
        .astype(jnp.bfloat16)
        .reshape(local_blocks, BLOCK, -1)
    )
    value_rows = (
        jnp.dot(inputs, w_value, preferred_element_type=jnp.float32)
        .astype(jnp.bfloat16)
        .reshape(local_blocks, BLOCK, -1)
    )
    all_keys, all_values = (
        lax.all_gather(key_rows, "seq", axis=0, tiled=True),
        lax.all_gather(value_rows, "seq", axis=0, tiled=True),
    )
    slab_blocks = all_keys.shape[0]
    first_block = lax.axis_index("seq") * local_blocks
    lists_all = neighbour_lists[0]
    counts_all = neighbour_counts[0]
    my_lists = lax.dynamic_slice_in_dim(lists_all, first_block, local_blocks, 0)
    my_counts = lax.dynamic_slice_in_dim(counts_all, first_block, local_blocks, 0)
    slot_keys = split_heads(
        jnp.take(all_keys, my_lists, axis=0).reshape(local_blocks, MAXN * BLOCK, -1)
    )
    slot_values = split_heads(
        jnp.take(all_values, my_lists, axis=0).reshape(local_blocks, MAXN * BLOCK, -1)
    )
    query_heads = split_heads(queries)
    scores = (
        jnp.einsum("bqhd,bkhd->bhqk", query_heads, slot_keys, preferred_element_type=jnp.float32)
        * score_scale
    )
    live_cols = (jnp.arange(MAXN * BLOCK) // BLOCK)[None, :] < my_counts[:, None]
    scores = jnp.where(live_cols[:, None, None, :], scores, -1e30)
    row_max = jnp.max(scores, axis=-1)
    exponent = jnp.exp(scores - row_max[..., None])
    totals = jnp.sum(exponent, axis=-1)
    mixed = jnp.einsum(
        "bhqk,bkhd->bqhd",
        exponent.astype(jnp.bfloat16),
        slot_values,
        preferred_element_type=jnp.float32,
    )
    attended = (
        (mixed / jnp.transpose(totals, (0, 2, 1))[..., None])
        .astype(jnp.bfloat16)
        .reshape(row_count, -1)
    )
    output = lax.dot_general(
        attended, w_out, (((1,), (1,)), ((), ())), preferred_element_type=jnp.float32
    ).astype(jnp.bfloat16)
    d_attended = jnp.dot(upstream, w_out, preferred_element_type=jnp.float32).astype(jnp.bfloat16)
    grad_out = lax.dot_general(
        upstream, attended, (((0,), (0,)), ((), ())), preferred_element_type=jnp.float32
    )
    d_blocks = d_attended.reshape(local_blocks, BLOCK, -1)
    d_heads = split_heads(d_blocks)
    attended_heads = split_heads(attended.reshape(local_blocks, BLOCK, -1))
    row_delta = jnp.transpose(
        jnp.sum(d_heads.astype(jnp.float32) * attended_heads.astype(jnp.float32), axis=-1),
        (0, 2, 1),
    )
    normed = exponent / totals[..., None]
    d_probs = jnp.einsum(
        "bqhd,bkhd->bhqk", d_heads, slot_values, preferred_element_type=jnp.float32
    )
    d_scores = (normed * (d_probs - row_delta[..., None])).astype(jnp.bfloat16)
    d_queries = (
        (
            jnp.einsum("bhqk,bkhd->bqhd", d_scores, slot_keys, preferred_element_type=jnp.float32)
            * score_scale
        )
        .astype(jnp.bfloat16)
        .reshape(row_count, -1)
    )
    gathered_query, gathered_dattn = (
        lax.all_gather(queries, "seq", axis=0, tiled=True),
        lax.all_gather(d_blocks, "seq", axis=0, tiled=True),
    )
    gathered_max, gathered_total, gathered_delta = (
        lax.all_gather(row_max, "seq", axis=0, tiled=True),
        lax.all_gather(totals, "seq", axis=0, tiled=True),
        lax.all_gather(row_delta, "seq", axis=0, tiled=True),
    )
    owners = first_block + jnp.arange(local_blocks)
    live_slots = jnp.arange(MAXN)[None, :] < counts_all[:, None]
    listed = jnp.any(
        (lists_all[:, :, None] == owners[None, None, :]) & live_slots[:, :, None], axis=1
    )
    groups = slab_blocks // 8
    own_keys = split_heads(key_rows)
    own_values = split_heads(value_rows)

    def regroup(matrix):
        return matrix.reshape((groups, 8) + matrix.shape[1:])

    def accumulate(carry, group_data):
        group_query, group_dattn, group_max, group_total, group_delta, group_listed = group_data
        group_query = split_heads(group_query)
        group_dattn = split_heads(group_dattn)
        group_scores = (
            jnp.einsum(
                "cqhd,ikhd->cihqk", group_query, own_keys, preferred_element_type=jnp.float32
            )
            * score_scale
        )
        group_scores = jnp.where(group_listed[:, :, None, None, None], group_scores, -1e30)
        group_probs = (
            jnp.exp(group_scores - group_max[:, None, :, :, None])
            / group_total[:, None, :, :, None]
        )
        group_dprobs = jnp.einsum(
            "cqhd,ikhd->cihqk", group_dattn, own_values, preferred_element_type=jnp.float32
        )
        group_dscores = (group_probs * (group_dprobs - group_delta[:, None, :, :, None])).astype(
            jnp.bfloat16
        )
        key_next = carry[0] + jnp.einsum(
            "cihqk,cqhd->ikhd", group_dscores, group_query, preferred_element_type=jnp.float32
        )
        value_next = carry[1] + jnp.einsum(
            "cihqk,cqhd->ikhd",
            group_probs.astype(jnp.bfloat16),
            group_dattn,
            preferred_element_type=jnp.float32,
        )
        return ((key_next, value_next), None)

    zero_sum = jnp.zeros((local_blocks, BLOCK, HEADS, HEAD_DIM), jnp.float32)
    group_inputs = (
        regroup(gathered_query),
        regroup(gathered_dattn),
        regroup(gathered_max),
        regroup(gathered_total),
        regroup(gathered_delta),
        regroup(listed),
    )
    (key_heads, value_heads), _ = lax.scan(accumulate, (zero_sum, zero_sum), group_inputs)
    key_sum = (key_heads * score_scale).reshape(local_blocks, BLOCK, -1)
    value_sum = value_heads.reshape(local_blocks, BLOCK, -1)
    d_keys = key_sum.astype(jnp.bfloat16).reshape(row_count, -1)
    d_values = value_sum.astype(jnp.bfloat16).reshape(row_count, -1)
    stacked = jnp.concatenate([d_queries, d_keys, d_values], axis=1)
    w_joined = jnp.concatenate([w_query, w_key, w_value], axis=1)
    d_inputs = lax.dot_general(
        stacked, w_joined, (((1,), (1,)), ((), ())), preferred_element_type=jnp.float32
    ).astype(jnp.bfloat16)
    grad_joined = lax.dot_general(
        inputs, stacked, (((0,), (0,)), ((), ())), preferred_element_type=jnp.float32
    )
    width_model = inputs.shape[1]
    grad_three = jnp.transpose(grad_joined.reshape(width_model, 3, -1), (1, 0, 2))
    grads = jnp.concatenate([grad_three, grad_out[None]], axis=0)
    within_slab = lax.psum_scatter(
        grads.astype(jnp.bfloat16), "seq", scatter_dimension=1, tiled=True
    )
    summed = lax.psum_scatter(within_slab, "rep", scatter_dimension=1, tiled=True).astype(
        jnp.float32
    )
    return (output[None], d_inputs[None], summed)


def solution(mesh):
    placed = (
        P("rep", "seq", None),
        P("rep", "seq", None),
        P(),
        P("rep", None, None),
        P("rep", None),
    )
    n, reps = mesh.shape["seq"], mesh.shape["rep"]
    run = functools.partial(by_heads, n, reps) if n == HEADS else body
    return jax.shard_map(
        run,
        mesh=mesh,
        in_specs=placed,
        out_specs=(P("rep", "seq", None), P("rep", "seq", None), P(None, ("seq", "rep"), None)),
        check_vma=False,
    )
```

```python
import functools
import math

import jax
import jax.numpy as jnp
from jax import lax
from jax.experimental import pallas as pl
from jax.experimental.pallas import tpu as pltpu
from jax.sharding import PartitionSpec as P

HEADS = 8
HEAD_DIM = 64
BLOCK = 128
MAXN = 27


F32 = jnp.float32
BF16 = jnp.bfloat16


def mm(a, b):
    return jnp.dot(a, b, preferred_element_type=F32)


def mm_nt(a, b):
    return lax.dot_general(a, b, (((1,), (1,)), ((), ())), preferred_element_type=F32)


def layer_kernel(
    n, reps,
    tok_hbm, cot_hbm, w_hbm, lists, counts,
    out, dinp, grads,
    tok, cot, w, send1, recv1, tstage, trecv, kt, vt, qtr, dtr, kx, vx, dkt, dvt, bias,
    normed_all, att_all, dq_all, xp, bk, back, gs, gr,
    ls, ss1, rs1, sst, rst, srl, ssb, rsb, ssp, rsp, ssg, rsg,
):
    me = lax.axis_index("seq")
    rep = lax.axis_index("rep")
    core = lax.rem(me, 2)
    chip = me // 2
    chips = n // 2
    scale = 1.0 / math.sqrt(HEAD_DIM)
    hd = HEAD_DIM
    part = gs.shape[2]

    loads = [
        pltpu.make_async_copy(cot_hbm.at[0], cot, ls.at[0]),
        pltpu.make_async_copy(tok_hbm.at[0], tok, ls.at[1]),
    ] + [pltpu.make_async_copy(w_hbm.at[j], w.at[j], ls.at[2 + j]) for j in range(4)]
    for load in loads:
        load.start()

    def remote(src, dst, s_sem, r_sem, seq, z):
        return pltpu.make_async_remote_copy(
            src_ref=src, dst_ref=dst, send_sem=s_sem, recv_sem=r_sem,
            device_id={"seq": seq, "rep": z}, device_id_type=pl.DeviceIdType.MESH,
        )

    barrier = pltpu.get_barrier_semaphore()

    def greet_seq(i, carry):
        pl.semaphore_signal(
            barrier, inc=1, device_id={"seq": lax.rem(me + i, n), "rep": rep},
            device_id_type=pl.DeviceIdType.MESH,
        )
        return carry

    def greet_rep(i, carry):
        pl.semaphore_signal(
            barrier, inc=1,
            device_id={
                "seq": lax.rem(me + 2 * lax.rem(i, chips), n),
                "rep": lax.rem(rep + 1 + i // chips, reps),
            },
            device_id_type=pl.DeviceIdType.MESH,
        )
        return carry

    lax.fori_loop(1, n, greet_seq, 0)
    lax.fori_loop(0, (reps - 1) * chips, greet_rep, 0)

    def each_peer(act):
        def step(i, carry):
            act(lax.rem(me + i, n))
            return carry

        lax.fori_loop(1, n, step, 0)

    x_chip = chip + 1 - 2 * lax.rem(chip, 2)
    y_chip = chip + 2 - 4 * (chip // 2)
    far_chip = chips - 1 - chip
    other = me + 1 - 2 * core

    def stage_cols(kind, ref):
        for s in range(n):
            cols = slice((s // 2) * BLOCK, (s // 2 + 1) * BLOCK)
            tstage[s % 2, kind, :, cols] = ref[:, s * BLOCK : (s + 1) * BLOCK]

    def cols_out(to, kind):
        return remote(
            tstage.at[lax.rem(to, 2), kind], trecv.at[me, kind],
            sst.at[kind, to], rst.at[kind, me], to, rep,
        )

    def cols_in(src, kind):
        return remote(
            tstage.at[core, kind], trecv.at[src, kind],
            sst.at[kind, src], rst.at[kind, src], src, rep,
        )

    def cols_on(kind, k):
        src, to = (y_chip, x_chip) if kind == 0 else (x_chip, y_chip)
        block = 2 * src + k
        return remote(
            trecv.at[block, kind], trecv.at[block, kind],
            srl.at[kind, k], rst.at[kind, block], 2 * to + core, rep,
        )

    def near(kind, act):
        act(other, kind)
        for k in range(2):
            act(2 * x_chip + k, kind)
            act(2 * y_chip + k, kind)

    def forward_cols(kind):
        for k in range(2):
            cols_in(2 * (y_chip if kind == 0 else x_chip) + k, kind).wait_recv()
            cols_on(kind, k).start()

    def finish_cols(kind):
        cols_in(other, kind).wait_recv()
        for k in range(2):
            cols_in(2 * (x_chip if kind == 0 else y_chip) + k, kind).wait_recv()
            cols_in(2 * far_chip + k, kind).wait_recv()

    loads[0].wait()
    stage_cols(1, cot)
    pl.semaphore_wait(barrier, n - 1 + (reps - 1) * chips)
    near(1, lambda to, kind: cols_out(to, kind).start())
    loads[1].wait()
    stage_cols(0, tok)

    def heads_out(to, piece):
        return remote(
            send1.at[to, piece], recv1.at[me, piece],
            ss1.at[piece, to], rs1.at[piece, me], to, rep,
        )

    def heads_in(src, piece):
        return remote(
            send1.at[src, piece], recv1.at[src, piece],
            ss1.at[piece, src], rs1.at[piece, src], src, rep,
        )

    def pack(piece, one, two):
        for h in range(n):
            cols = slice(h * hd, (h + 1) * hd)
            send1[h, piece] = jnp.concatenate([one[:, cols], two[:, cols]], axis=1)
        each_peer(lambda to: heads_out(to, piece).start())
        recv1[me, piece] = send1[me, piece]

    x = tok[...]
    loads[2].wait()
    q = (mm(x, w[0]).astype(BF16).astype(F32) * scale).astype(BF16)
    loads[3].wait()
    k = mm(x, w[1]).astype(BF16)
    pack(0, q, k)
    loads[4].wait()
    v = mm(x, w[2]).astype(BF16)
    loads[5].wait()
    da = mm(cot[...], w[3]).astype(BF16)
    pack(1, v, da)

    near(0, lambda to, kind: cols_out(to, kind).start())
    trecv[pl.ds(me, 1)] = tstage[pl.ds(core, 1)]

    eye = lax.broadcasted_iota(jnp.int32, (n, n), 0) == lax.broadcasted_iota(jnp.int32, (n, n), 1)
    count_col = jnp.sum(
        jnp.where(eye, jnp.broadcast_to(counts[...].astype(F32), (n, n)), 0.0),
        axis=1, keepdims=True,
    )
    listed = lists[0]
    slot = lax.broadcasted_iota(jnp.int32, listed.shape, 1).astype(F32)
    alive = slot < count_col
    for c in range(n):
        hit = jnp.max(
            jnp.where(jnp.logical_and(listed == c, alive), 1.0, 0.0), axis=1, keepdims=True
        )
        bias[:, c * BLOCK : (c + 1) * BLOCK] = jnp.broadcast_to((hit - 1.0) * 1e30, (n, BLOCK))
    dkt[...] = jnp.zeros_like(dkt)
    dvt[...] = jnp.zeros_like(dvt)

    each_peer(lambda src: heads_in(src, 0).wait_recv())
    for b in range(n):
        rows = slice(b * BLOCK, (b + 1) * BLOCK)
        qk = recv1[b, 0]
        kx[rows] = qk[:, hd:]
        qkt = qk.T
        qtr[:, rows] = qkt[:hd]
        kt[:, rows] = qkt[hd:]
    each_peer(lambda src: heads_in(src, 1).wait_recv())
    for b in range(n):
        rows = slice(b * BLOCK, (b + 1) * BLOCK)
        vd = recv1[b, 1]
        vx[rows] = vd[:, :hd]
        vdt = vd.T
        vt[:, rows] = vdt[:hd]
        dtr[:, rows] = vdt[hd:]

    forward_cols(1)

    def back_out(b, piece):
        rows = pl.ds(pl.multiple_of(b * BLOCK, BLOCK), BLOCK)
        return remote(
            bk.at[piece, rows], back.at[me, piece],
            ssb.at[piece, b], rsb.at[piece, me], b, rep,
        )

    def back_in(h, piece):
        return remote(
            bk.at[piece, pl.ds(0, BLOCK)], back.at[h, piece],
            ssb.at[piece, h], rsb.at[piece, h], h, rep,
        )

    def pair_out(piece):
        return remote(
            xp.at[core, piece], xp.at[core, piece], ssp.at[piece], rsp.at[piece], other, rep
        )

    def pair_in(piece):
        return remote(
            xp.at[1 - core, piece], xp.at[1 - core, piece],
            ssp.at[piece], rsp.at[piece], other, rep,
        )

    def pair_of(i):
        return pl.ds(pl.multiple_of(2 * i * BLOCK, 2 * BLOCK), 2 * BLOCK)

    def two_blocks(i, piece):
        return recv1[pl.ds(2 * i, 2), piece].reshape(2 * BLOCK, 2 * hd)

    def forward(i, carry):
        rows = pair_of(i)
        mask = [
            jnp.broadcast_to(bias[pl.ds(2 * i + j, 1), :], (BLOCK, n * BLOCK)) for j in range(2)
        ]
        s = mm(two_blocks(i, 0)[:, :hd], kt[...]) + jnp.concatenate(mask, axis=0)
        e = jnp.exp(s - jnp.max(s, axis=1, keepdims=True))
        total = jnp.sum(e, axis=1, keepdims=True)
        att = (mm(e.astype(BF16), vx[...]) / total).astype(BF16)
        att_all[rows] = att
        xp[core, 0, :hd, rows] = att.T
        normed = e * (1.0 / total)
        normed_all[rows] = normed
        dvt[...] += mm(dtr[:, rows], normed.astype(BF16))
        return carry

    lax.fori_loop(0, n // 2, forward, 0, unroll=2)
    xp[core, 0, hd:] = dvt[...].astype(BF16)
    pair_out(0).start()

    for b in range(n):
        rows = slice(b * BLOCK, (b + 1) * BLOCK)
        bk[0, rows] = jnp.concatenate([att_all[rows], dvt[:, rows].T.astype(BF16)], axis=1)
    each_peer(lambda to: back_out(to, 0).start())
    forward_cols(0)

    def backward(i, carry):
        rows = pair_of(i)
        dab = two_blocks(i, 1)[:, hd:]
        delta = jnp.sum(dab.astype(F32) * att_all[rows].astype(F32), axis=1, keepdims=True)
        ds = (normed_all[rows] * (mm(dab, vt[...]) - delta)).astype(BF16)
        dkt[...] += mm(qtr[:, rows], ds)
        dq = (mm(ds, kx[...]) * scale).astype(BF16)
        dq_all[rows] = dq
        xp[core, 1, :hd, rows] = dq.T
        return carry

    def grads_out(i, k0, count, stage):
        chip_to = lax.rem(chip + i, chips)
        rep_to = lax.rem(rep + i // chips, reps)
        to = chip_to * reps + rep_to
        here = chip * reps + rep
        return remote(
            gs.at[to, pl.ds(k0, count)], gr.at[here, pl.ds(k0, count)],
            ssg.at[stage, to], rsg.at[stage, here], 2 * chip_to + core, rep_to,
        )

    def grads_in(i, k0, count, stage):
        chip_from = lax.rem(chip + i, chips)
        rep_from = lax.rem(rep + i // chips, reps)
        src = chip_from * reps + rep_from
        return remote(
            gs.at[src, pl.ds(k0, count)], gr.at[src, pl.ds(k0, count)],
            ssg.at[stage, src], rsg.at[stage, src], 2 * chip_from + core, rep_from,
        )

    stages = ((3, 1, 0), (2, 1, 1), (0, 2, 2))

    def each_group(act):
        def step(i, carry):
            act(i)
            return carry

        lax.fori_loop(1, chips * reps, step, 0)

    def product(kinds, column_kind, piece, rows):
        left = jnp.concatenate(
            [xp[c, piece][r] for r in rows for c in range(2)], axis=0
        )
        right = trecv[:, column_kind].reshape(n * BLOCK, trecv.shape[3])
        total = mm(left, right).astype(BF16)
        for j, kind in enumerate(kinds):
            one = total[2 * hd * j : 2 * hd * (j + 1)].T
            gs[:, kind] = one.reshape(chips * reps, part, 2 * hd)

    low, high = slice(0, hd), slice(hd, 2 * hd)
    lax.fori_loop(0, 2, backward, 0, unroll=2)
    finish_cols(1)
    pair_in(0).wait_recv()
    product((3,), 1, 0, (low,))
    each_group(lambda i: grads_out(i, *stages[0]).start())
    lax.fori_loop(2, n // 2, backward, 0, unroll=2)

    xp[core, 1, hd:] = dkt[...].astype(BF16)
    pair_out(1).start()
    finish_cols(0)
    product((2,), 0, 0, (high,))
    each_group(lambda i: grads_out(i, *stages[1]).start())
    pair_in(1).wait_recv()
    product((0, 1), 0, 1, (low, high))
    each_group(lambda i: grads_out(i, *stages[2]).start())
    gr[pl.ds(chip * reps + rep, 1)] = gs[pl.ds(chip * reps + rep, 1)]

    for b in range(n):
        rows = slice(b * BLOCK, (b + 1) * BLOCK)
        bk[1, rows] = jnp.concatenate([dq_all[rows], dkt[:, rows].T.astype(BF16)], axis=1)
    each_peer(lambda to: back_out(to, 1).start())
    mine = pl.ds(pl.multiple_of(me * BLOCK, BLOCK), BLOCK)
    for piece in range(2):
        back[me, piece] = bk[piece, mine]

    each_peer(lambda src: back_in(src, 0).wait_recv())
    att = jnp.concatenate([back[h, 0][:, :hd] for h in range(n)], axis=1)
    dv = jnp.concatenate([back[h, 0][:, hd:] for h in range(n)], axis=1)
    out[0] = mm_nt(att, w[3]).astype(BF16)
    each_peer(lambda src: back_in(src, 1).wait_recv())
    dq = jnp.concatenate([back[h, 1][:, :hd] for h in range(n)], axis=1)
    dk = jnp.concatenate([back[h, 1][:, hd:] for h in range(n)], axis=1)
    dinp[0] = (mm_nt(dq, w[0]) + mm_nt(dk, w[1]) + mm_nt(dv, w[2])).astype(BF16)

    def drain(to):
        for piece in range(2):
            heads_out(to, piece).wait_send()
            back_out(to, piece).wait_send()

    each_peer(drain)
    for kind in range(2):
        near(kind, lambda to, kind: cols_out(to, kind).wait_send())
        for k in range(2):
            cols_on(kind, k).wait_send()
    pair_out(0).wait_send()
    pair_out(1).wait_send()
    for stage in stages:
        each_group(lambda i, stage=stage: grads_out(i, *stage).wait_send())
        each_group(lambda i, stage=stage: grads_in(i, *stage).wait_recv())
        kinds = slice(stage[0], stage[0] + stage[1])
        for c in range(chips):
            acc = gr[c * reps, kinds].astype(F32)
            for r in range(1, reps):
                acc = acc + gr[c * reps + r, kinds].astype(F32)
            grads[kinds, :, c * 2 * hd : (c + 1) * 2 * hd] = acc


def by_heads(n, reps, tokens, cotangent, weights, neighbour_lists, neighbour_counts):
    width = tokens.shape[2]
    slab = n * BLOCK
    cols = weights.shape[2]
    part = width // (n * reps)
    groups = (n // 2) * reps
    vmem = pl.BlockSpec(memory_space=pltpu.VMEM)
    hbm = pl.BlockSpec(memory_space=pl.ANY)
    dma = pltpu.SemaphoreType.DMA
    return pl.pallas_call(
        functools.partial(layer_kernel, n, reps),
        out_shape=(
            jax.ShapeDtypeStruct(tokens.shape, BF16),
            jax.ShapeDtypeStruct(tokens.shape, BF16),
            jax.ShapeDtypeStruct((4, part, cols), F32),
        ),
        in_specs=[hbm] * 3 + [vmem] * 2,
        out_specs=(vmem, vmem, vmem),
        scratch_shapes=[
            pltpu.VMEM((BLOCK, width), BF16),
            pltpu.VMEM((BLOCK, width), BF16),
            pltpu.VMEM(weights.shape, BF16),
            pltpu.VMEM((n, 2, BLOCK, 2 * HEAD_DIM), BF16),
            pltpu.VMEM((n, 2, BLOCK, 2 * HEAD_DIM), BF16),
            pltpu.VMEM((2, 2, BLOCK, width // 2), BF16),
            pltpu.VMEM((n, 2, BLOCK, width // 2), BF16),
            pltpu.VMEM((HEAD_DIM, slab), BF16),
            pltpu.VMEM((HEAD_DIM, slab), BF16),
            pltpu.VMEM((HEAD_DIM, slab), BF16),
            pltpu.VMEM((HEAD_DIM, slab), BF16),
            pltpu.VMEM((slab, HEAD_DIM), BF16),
            pltpu.VMEM((slab, HEAD_DIM), BF16),
            pltpu.VMEM((HEAD_DIM, slab), F32),
            pltpu.VMEM((HEAD_DIM, slab), F32),
            pltpu.VMEM((n, slab), F32),
            pltpu.VMEM((slab, slab), F32),
            pltpu.VMEM((slab, HEAD_DIM), BF16),
            pltpu.VMEM((slab, HEAD_DIM), BF16),
            pltpu.VMEM((2, 2, 2 * HEAD_DIM, slab), BF16),
            pltpu.VMEM((2, slab, 2 * HEAD_DIM), BF16),
            pltpu.VMEM((n, 2, BLOCK, 2 * HEAD_DIM), BF16),
            pltpu.VMEM((groups, 4, part, 2 * HEAD_DIM), BF16),
            pltpu.VMEM((groups, 4, part, 2 * HEAD_DIM), BF16),
            dma((6,)),
            dma((2, n)), dma((2, n)), dma((2, n)), dma((2, n)), dma((2, 2)),
            dma((2, n)), dma((2, n)),
            dma((2,)), dma((2,)), dma((3, groups)), dma((3, groups)),
        ],
        compiler_params=pltpu.CompilerParams(
            collective_id=0, has_side_effects=True, vmem_limit_bytes=53 * 1024 * 1024
        ),
        cost_estimate=pl.CostEstimate(
            flops=3 * 10**9, bytes_accessed=6 * 2**20, transcendentals=2**20
        ),
    )(tokens, cotangent, weights, neighbour_lists, neighbour_counts)


def split_heads(matrix):
    return matrix.reshape(matrix.shape[:-1] + (HEADS, HEAD_DIM))


def body(tokens, cotangent, weights, neighbour_lists, neighbour_counts):
    score_scale = 1.0 / math.sqrt(HEAD_DIM)
    inputs = tokens[0]
    upstream = cotangent[0]
    row_count = inputs.shape[0]
    local_blocks = row_count // BLOCK
    w_query, w_key, w_value, w_out = (weights[0], weights[1], weights[2], weights[3])
    queries = (
        jnp.dot(inputs, w_query, preferred_element_type=jnp.float32)
        .astype(jnp.bfloat16)
        .reshape(local_blocks, BLOCK, -1)
    )
    key_rows = (
        jnp.dot(inputs, w_key, preferred_element_type=jnp.float32)
        .astype(jnp.bfloat16)
        .reshape(local_blocks, BLOCK, -1)
    )
    value_rows = (
        jnp.dot(inputs, w_value, preferred_element_type=jnp.float32)
        .astype(jnp.bfloat16)
        .reshape(local_blocks, BLOCK, -1)
    )
    all_keys, all_values = (
        lax.all_gather(key_rows, "seq", axis=0, tiled=True),
        lax.all_gather(value_rows, "seq", axis=0, tiled=True),
    )
    slab_blocks = all_keys.shape[0]
    first_block = lax.axis_index("seq") * local_blocks
    lists_all = neighbour_lists[0]
    counts_all = neighbour_counts[0]
    my_lists = lax.dynamic_slice_in_dim(lists_all, first_block, local_blocks, 0)
    my_counts = lax.dynamic_slice_in_dim(counts_all, first_block, local_blocks, 0)
    slot_keys = split_heads(
        jnp.take(all_keys, my_lists, axis=0).reshape(local_blocks, MAXN * BLOCK, -1)
    )
    slot_values = split_heads(
        jnp.take(all_values, my_lists, axis=0).reshape(local_blocks, MAXN * BLOCK, -1)
    )
    query_heads = split_heads(queries)
    scores = (
        jnp.einsum("bqhd,bkhd->bhqk", query_heads, slot_keys, preferred_element_type=jnp.float32)
        * score_scale
    )
    live_cols = (jnp.arange(MAXN * BLOCK) // BLOCK)[None, :] < my_counts[:, None]
    scores = jnp.where(live_cols[:, None, None, :], scores, -1e30)
    row_max = jnp.max(scores, axis=-1)
    exponent = jnp.exp(scores - row_max[..., None])
    totals = jnp.sum(exponent, axis=-1)
    mixed = jnp.einsum(
        "bhqk,bkhd->bqhd",
        exponent.astype(jnp.bfloat16),
        slot_values,
        preferred_element_type=jnp.float32,
    )
    attended = (
        (mixed / jnp.transpose(totals, (0, 2, 1))[..., None])
        .astype(jnp.bfloat16)
        .reshape(row_count, -1)
    )
    output = lax.dot_general(
        attended, w_out, (((1,), (1,)), ((), ())), preferred_element_type=jnp.float32
    ).astype(jnp.bfloat16)
    d_attended = jnp.dot(upstream, w_out, preferred_element_type=jnp.float32).astype(jnp.bfloat16)
    grad_out = lax.dot_general(
        upstream, attended, (((0,), (0,)), ((), ())), preferred_element_type=jnp.float32
    )
    d_blocks = d_attended.reshape(local_blocks, BLOCK, -1)
    d_heads = split_heads(d_blocks)
    attended_heads = split_heads(attended.reshape(local_blocks, BLOCK, -1))
    row_delta = jnp.transpose(
        jnp.sum(d_heads.astype(jnp.float32) * attended_heads.astype(jnp.float32), axis=-1),
        (0, 2, 1),
    )
    normed = exponent / totals[..., None]
    d_probs = jnp.einsum(
        "bqhd,bkhd->bhqk", d_heads, slot_values, preferred_element_type=jnp.float32
    )
    d_scores = (normed * (d_probs - row_delta[..., None])).astype(jnp.bfloat16)
    d_queries = (
        (
            jnp.einsum("bhqk,bkhd->bqhd", d_scores, slot_keys, preferred_element_type=jnp.float32)
            * score_scale
        )
        .astype(jnp.bfloat16)
        .reshape(row_count, -1)
    )
    gathered_query, gathered_dattn = (
        lax.all_gather(queries, "seq", axis=0, tiled=True),
        lax.all_gather(d_blocks, "seq", axis=0, tiled=True),
    )
    gathered_max, gathered_total, gathered_delta = (
        lax.all_gather(row_max, "seq", axis=0, tiled=True),
        lax.all_gather(totals, "seq", axis=0, tiled=True),
        lax.all_gather(row_delta, "seq", axis=0, tiled=True),
    )
    owners = first_block + jnp.arange(local_blocks)
    live_slots = jnp.arange(MAXN)[None, :] < counts_all[:, None]
    listed = jnp.any(
        (lists_all[:, :, None] == owners[None, None, :]) & live_slots[:, :, None], axis=1
    )
    groups = slab_blocks // 8
    own_keys = split_heads(key_rows)
    own_values = split_heads(value_rows)

    def regroup(matrix):
        return matrix.reshape((groups, 8) + matrix.shape[1:])

    def accumulate(carry, group_data):
        group_query, group_dattn, group_max, group_total, group_delta, group_listed = group_data
        group_query = split_heads(group_query)
        group_dattn = split_heads(group_dattn)
        group_scores = (
            jnp.einsum(
                "cqhd,ikhd->cihqk", group_query, own_keys, preferred_element_type=jnp.float32
            )
            * score_scale
        )
        group_scores = jnp.where(group_listed[:, :, None, None, None], group_scores, -1e30)
        group_probs = (
            jnp.exp(group_scores - group_max[:, None, :, :, None])
            / group_total[:, None, :, :, None]
        )
        group_dprobs = jnp.einsum(
            "cqhd,ikhd->cihqk", group_dattn, own_values, preferred_element_type=jnp.float32
        )
        group_dscores = (group_probs * (group_dprobs - group_delta[:, None, :, :, None])).astype(
            jnp.bfloat16
        )
        key_next = carry[0] + jnp.einsum(
            "cihqk,cqhd->ikhd", group_dscores, group_query, preferred_element_type=jnp.float32
        )
        value_next = carry[1] + jnp.einsum(
            "cihqk,cqhd->ikhd",
            group_probs.astype(jnp.bfloat16),
            group_dattn,
            preferred_element_type=jnp.float32,
        )
        return ((key_next, value_next), None)

    zero_sum = jnp.zeros((local_blocks, BLOCK, HEADS, HEAD_DIM), jnp.float32)
    group_inputs = (
        regroup(gathered_query),
        regroup(gathered_dattn),
        regroup(gathered_max),
        regroup(gathered_total),
        regroup(gathered_delta),
        regroup(listed),
    )
    (key_heads, value_heads), _ = lax.scan(accumulate, (zero_sum, zero_sum), group_inputs)
    key_sum = (key_heads * score_scale).reshape(local_blocks, BLOCK, -1)
    value_sum = value_heads.reshape(local_blocks, BLOCK, -1)
    d_keys = key_sum.astype(jnp.bfloat16).reshape(row_count, -1)
    d_values = value_sum.astype(jnp.bfloat16).reshape(row_count, -1)
    stacked = jnp.concatenate([d_queries, d_keys, d_values], axis=1)
    w_joined = jnp.concatenate([w_query, w_key, w_value], axis=1)
    d_inputs = lax.dot_general(
        stacked, w_joined, (((1,), (1,)), ((), ())), preferred_element_type=jnp.float32
    ).astype(jnp.bfloat16)
    grad_joined = lax.dot_general(
        inputs, stacked, (((0,), (0,)), ((), ())), preferred_element_type=jnp.float32
    )
    width_model = inputs.shape[1]
    grad_three = jnp.transpose(grad_joined.reshape(width_model, 3, -1), (1, 0, 2))
    grads = jnp.concatenate([grad_three, grad_out[None]], axis=0)
    within_slab = lax.psum_scatter(
        grads.astype(jnp.bfloat16), "seq", scatter_dimension=1, tiled=True
    )
    summed = lax.psum_scatter(within_slab, "rep", scatter_dimension=1, tiled=True).astype(
        jnp.float32
    )
    return (output[None], d_inputs[None], summed)


def solution(mesh):
    placed = (
        P("rep", "seq", None),
        P("rep", "seq", None),
        P(),
        P("rep", None, None),
        P("rep", None),
    )
    n, reps = mesh.shape["seq"], mesh.shape["rep"]
    run = functools.partial(by_heads, n, reps) if n == HEADS else body
    return jax.shard_map(
        run,
        mesh=mesh,
        in_specs=placed,
        out_specs=(P("rep", "seq", None), P("rep", "seq", None), P(None, ("seq", "rep"), None)),
        check_vma=False,
    )
```

```python
import functools
import math

import jax
import jax.numpy as jnp
from jax import lax
from jax.experimental import pallas as pl
from jax.experimental.pallas import tpu as pltpu
from jax.sharding import PartitionSpec as P

HEADS = 8
HEAD_DIM = 64
BLOCK = 128
MAXN = 27


F32 = jnp.float32
BF16 = jnp.bfloat16


def mm(a, b):
    return jnp.dot(a, b, preferred_element_type=F32)


def mm_nt(a, b):
    return lax.dot_general(a, b, (((1,), (1,)), ((), ())), preferred_element_type=F32)


def layer_kernel(
    n, reps,
    tok_hbm, cot_hbm, w_hbm, lists, counts,
    out, dinp, grads,
    tok, cot, w, send1, recv1, tstage, trecv, kt, vt, qtr, dtr, kx, vx, dkt, dvt, bias,
    normed_all, att_all, dq_all, xp, bk, back, gs, gr,
    ls, ss1, rs1, sst, rst, srl, ssb, rsb, ssp, rsp, ssg, rsg,
):
    me = lax.axis_index("seq")
    rep = lax.axis_index("rep")
    core = lax.rem(me, 2)
    chip = me // 2
    chips = n // 2
    scale = 1.0 / math.sqrt(HEAD_DIM)
    hd = HEAD_DIM
    part = gs.shape[2]

    loads = [
        pltpu.make_async_copy(cot_hbm.at[0], cot, ls.at[0]),
        pltpu.make_async_copy(tok_hbm.at[0], tok, ls.at[1]),
    ] + [pltpu.make_async_copy(w_hbm.at[j], w.at[j], ls.at[2 + j]) for j in range(4)]
    for load in loads:
        load.start()

    def remote(src, dst, s_sem, r_sem, seq, z):
        return pltpu.make_async_remote_copy(
            src_ref=src, dst_ref=dst, send_sem=s_sem, recv_sem=r_sem,
            device_id={"seq": seq, "rep": z}, device_id_type=pl.DeviceIdType.MESH,
        )

    barrier = pltpu.get_barrier_semaphore()

    def greet_seq(i, carry):
        pl.semaphore_signal(
            barrier, inc=1, device_id={"seq": lax.rem(me + i, n), "rep": rep},
            device_id_type=pl.DeviceIdType.MESH,
        )
        return carry

    def greet_rep(i, carry):
        pl.semaphore_signal(
            barrier, inc=1,
            device_id={
                "seq": lax.rem(me + 2 * lax.rem(i, chips), n),
                "rep": lax.rem(rep + 1 + i // chips, reps),
            },
            device_id_type=pl.DeviceIdType.MESH,
        )
        return carry

    lax.fori_loop(1, n, greet_seq, 0)
    lax.fori_loop(0, (reps - 1) * chips, greet_rep, 0)

    def each_peer(act):
        def step(i, carry):
            act(lax.rem(me + i, n))
            return carry

        lax.fori_loop(1, n, step, 0)

    x_chip = chip + 1 - 2 * lax.rem(chip, 2)
    y_chip = chip + 2 - 4 * (chip // 2)
    far_chip = chips - 1 - chip
    other = me + 1 - 2 * core

    def stage_cols(kind, ref):
        for s in range(n):
            cols = slice((s // 2) * BLOCK, (s // 2 + 1) * BLOCK)
            tstage[s % 2, kind, :, cols] = ref[:, s * BLOCK : (s + 1) * BLOCK]

    def cols_out(to, kind):
        return remote(
            tstage.at[lax.rem(to, 2), kind], trecv.at[me, kind],
            sst.at[kind, to], rst.at[kind, me], to, rep,
        )

    def cols_in(src, kind):
        return remote(
            tstage.at[core, kind], trecv.at[src, kind],
            sst.at[kind, src], rst.at[kind, src], src, rep,
        )

    def cols_on(kind, k):
        src, to = (y_chip, x_chip) if kind == 0 else (x_chip, y_chip)
        block = 2 * src + k
        return remote(
            trecv.at[block, kind], trecv.at[block, kind],
            srl.at[kind, k], rst.at[kind, block], 2 * to + core, rep,
        )

    def near(kind, act):
        act(other, kind)
        for k in range(2):
            act(2 * x_chip + k, kind)
            act(2 * y_chip + k, kind)

    def forward_cols(kind):
        for k in range(2):
            cols_in(2 * (y_chip if kind == 0 else x_chip) + k, kind).wait_recv()
            cols_on(kind, k).start()

    def finish_cols(kind):
        cols_in(other, kind).wait_recv()
        for k in range(2):
            cols_in(2 * (x_chip if kind == 0 else y_chip) + k, kind).wait_recv()
            cols_in(2 * far_chip + k, kind).wait_recv()

    loads[0].wait()
    stage_cols(1, cot)
    pl.semaphore_wait(barrier, n - 1 + (reps - 1) * chips)
    near(1, lambda to, kind: cols_out(to, kind).start())
    loads[1].wait()
    stage_cols(0, tok)

    def heads_out(to, piece):
        return remote(
            send1.at[to, piece], recv1.at[me, piece],
            ss1.at[piece, to], rs1.at[piece, me], to, rep,
        )

    def heads_in(src, piece):
        return remote(
            send1.at[src, piece], recv1.at[src, piece],
            ss1.at[piece, src], rs1.at[piece, src], src, rep,
        )

    def pack(piece, one, two):
        for h in range(n):
            cols = slice(h * hd, (h + 1) * hd)
            send1[h, piece] = jnp.concatenate([one[:, cols], two[:, cols]], axis=1)
        each_peer(lambda to: heads_out(to, piece).start())
        recv1[me, piece] = send1[me, piece]

    x = tok[...]
    loads[2].wait()
    q = (mm(x, w[0]).astype(BF16).astype(F32) * scale).astype(BF16)
    loads[3].wait()
    k = mm(x, w[1]).astype(BF16)
    pack(0, q, k)
    loads[4].wait()
    v = mm(x, w[2]).astype(BF16)
    loads[5].wait()
    da = mm(cot[...], w[3]).astype(BF16)
    pack(1, v, da)

    trecv[pl.ds(me, 1)] = tstage[pl.ds(core, 1)]

    eye = lax.broadcasted_iota(jnp.int32, (n, n), 0) == lax.broadcasted_iota(jnp.int32, (n, n), 1)
    count_col = jnp.sum(
        jnp.where(eye, jnp.broadcast_to(counts[...].astype(F32), (n, n)), 0.0),
        axis=1, keepdims=True,
    )
    listed = lists[0]
    slot = lax.broadcasted_iota(jnp.int32, listed.shape, 1).astype(F32)
    alive = slot < count_col
    for c in range(n):
        hit = jnp.max(
            jnp.where(jnp.logical_and(listed == c, alive), 1.0, 0.0), axis=1, keepdims=True
        )
        bias[:, c * BLOCK : (c + 1) * BLOCK] = jnp.broadcast_to((hit - 1.0) * 1e30, (n, BLOCK))
    dkt[...] = jnp.zeros_like(dkt)
    dvt[...] = jnp.zeros_like(dvt)

    each_peer(lambda src: heads_in(src, 0).wait_recv())
    for b in range(n):
        rows = slice(b * BLOCK, (b + 1) * BLOCK)
        qk = recv1[b, 0]
        kx[rows] = qk[:, hd:]
        qkt = qk.T
        qtr[:, rows] = qkt[:hd]
        kt[:, rows] = qkt[hd:]
    forward_cols(1)
    near(0, lambda to, kind: cols_out(to, kind).start())

    def back_out(b, piece):
        rows = pl.ds(pl.multiple_of(b * BLOCK, BLOCK), BLOCK)
        return remote(
            bk.at[piece, rows], back.at[me, piece],
            ssb.at[piece, b], rsb.at[piece, me], b, rep,
        )

    def back_in(h, piece):
        return remote(
            bk.at[piece, pl.ds(0, BLOCK)], back.at[h, piece],
            ssb.at[piece, h], rsb.at[piece, h], h, rep,
        )

    def pair_out(piece):
        return remote(
            xp.at[core, piece], xp.at[core, piece], ssp.at[piece], rsp.at[piece], other, rep
        )

    def pair_in(piece):
        return remote(
            xp.at[1 - core, piece], xp.at[1 - core, piece],
            ssp.at[piece], rsp.at[piece], other, rep,
        )

    def pair_of(i):
        return pl.ds(pl.multiple_of(2 * i * BLOCK, 2 * BLOCK), 2 * BLOCK)

    def two_blocks(i, piece):
        return recv1[pl.ds(2 * i, 2), piece].reshape(2 * BLOCK, 2 * hd)

    def weigh(i, carry):
        rows = pair_of(i)
        mask = [
            jnp.broadcast_to(bias[pl.ds(2 * i + j, 1), :], (BLOCK, n * BLOCK)) for j in range(2)
        ]
        s = mm(two_blocks(i, 0)[:, :hd], kt[...]) + jnp.concatenate(mask, axis=0)
        e = jnp.exp(s - jnp.max(s, axis=1, keepdims=True))
        normed_all[rows] = e * (1.0 / jnp.sum(e, axis=1, keepdims=True))
        return carry

    def forward(i, carry):
        rows = pair_of(i)
        p = normed_all[rows].astype(BF16)
        att = mm(p, vx[...]).astype(BF16)
        att_all[rows] = att
        xp[core, 0, :hd, rows] = att.T
        dvt[...] += mm(dtr[:, rows], p)
        return carry

    lax.fori_loop(0, n // 2, weigh, 0, unroll=2)
    each_peer(lambda src: heads_in(src, 1).wait_recv())
    for b in range(n):
        rows = slice(b * BLOCK, (b + 1) * BLOCK)
        vd = recv1[b, 1]
        vx[rows] = vd[:, :hd]
        vdt = vd.T
        vt[:, rows] = vdt[:hd]
        dtr[:, rows] = vdt[hd:]

    lax.fori_loop(0, n // 2, forward, 0, unroll=2)
    xp[core, 0, hd:] = dvt[...].astype(BF16)
    pair_out(0).start()

    for b in range(n):
        rows = slice(b * BLOCK, (b + 1) * BLOCK)
        bk[0, rows] = jnp.concatenate([att_all[rows], dvt[:, rows].T.astype(BF16)], axis=1)
    each_peer(lambda to: back_out(to, 0).start())

    def backward(i, carry):
        rows = pair_of(i)
        dab = two_blocks(i, 1)[:, hd:]
        delta = jnp.sum(dab.astype(F32) * att_all[rows].astype(F32), axis=1, keepdims=True)
        ds = (normed_all[rows] * (mm(dab, vt[...]) - delta)).astype(BF16)
        dkt[...] += mm(qtr[:, rows], ds)
        dq = (mm(ds, kx[...]) * scale).astype(BF16)
        dq_all[rows] = dq
        xp[core, 1, :hd, rows] = dq.T
        return carry

    def grads_out(i, k0, count, stage):
        chip_to = lax.rem(chip + i, chips)
        rep_to = lax.rem(rep + i // chips, reps)
        to = chip_to * reps + rep_to
        here = chip * reps + rep
        return remote(
            gs.at[to, pl.ds(k0, count)], gr.at[here, pl.ds(k0, count)],
            ssg.at[stage, to], rsg.at[stage, here], 2 * chip_to + core, rep_to,
        )

    def grads_in(i, k0, count, stage):
        chip_from = lax.rem(chip + i, chips)
        rep_from = lax.rem(rep + i // chips, reps)
        src = chip_from * reps + rep_from
        return remote(
            gs.at[src, pl.ds(k0, count)], gr.at[src, pl.ds(k0, count)],
            ssg.at[stage, src], rsg.at[stage, src], 2 * chip_from + core, rep_from,
        )

    stages = ((3, 1, 0), (2, 1, 1), (0, 2, 2))

    def each_group(act):
        def step(i, carry):
            act(i)
            return carry

        lax.fori_loop(1, chips * reps, step, 0)

    def product(kinds, column_kind, piece, rows):
        left = jnp.concatenate(
            [xp[c, piece][r] for r in rows for c in range(2)], axis=0
        )
        right = trecv[:, column_kind].reshape(n * BLOCK, trecv.shape[3])
        total = mm(left, right).astype(BF16)
        for j, kind in enumerate(kinds):
            one = total[2 * hd * j : 2 * hd * (j + 1)].T
            gs[:, kind] = one.reshape(chips * reps, part, 2 * hd)

    low, high = slice(0, hd), slice(hd, 2 * hd)
    lax.fori_loop(0, 2, backward, 0, unroll=2)
    forward_cols(0)
    finish_cols(1)
    pair_in(0).wait_recv()
    product((3,), 1, 0, (low,))
    each_group(lambda i: grads_out(i, *stages[0]).start())
    lax.fori_loop(2, n // 2, backward, 0, unroll=2)

    xp[core, 1, hd:] = dkt[...].astype(BF16)
    pair_out(1).start()
    finish_cols(0)
    product((2,), 0, 0, (high,))
    each_group(lambda i: grads_out(i, *stages[1]).start())
    pair_in(1).wait_recv()
    product((0, 1), 0, 1, (low, high))
    each_group(lambda i: grads_out(i, *stages[2]).start())
    gr[pl.ds(chip * reps + rep, 1)] = gs[pl.ds(chip * reps + rep, 1)]

    for b in range(n):
        rows = slice(b * BLOCK, (b + 1) * BLOCK)
        bk[1, rows] = jnp.concatenate([dq_all[rows], dkt[:, rows].T.astype(BF16)], axis=1)
    each_peer(lambda to: back_out(to, 1).start())
    mine = pl.ds(pl.multiple_of(me * BLOCK, BLOCK), BLOCK)
    for piece in range(2):
        back[me, piece] = bk[piece, mine]

    each_peer(lambda src: back_in(src, 0).wait_recv())
    att = jnp.concatenate([back[h, 0][:, :hd] for h in range(n)], axis=1)
    dv = jnp.concatenate([back[h, 0][:, hd:] for h in range(n)], axis=1)
    out[0] = mm_nt(att, w[3]).astype(BF16)
    each_peer(lambda src: back_in(src, 1).wait_recv())
    dq = jnp.concatenate([back[h, 1][:, :hd] for h in range(n)], axis=1)
    dk = jnp.concatenate([back[h, 1][:, hd:] for h in range(n)], axis=1)
    dinp[0] = (mm_nt(dq, w[0]) + mm_nt(dk, w[1]) + mm_nt(dv, w[2])).astype(BF16)

    def drain(to):
        for piece in range(2):
            heads_out(to, piece).wait_send()
            back_out(to, piece).wait_send()

    each_peer(drain)
    for kind in range(2):
        near(kind, lambda to, kind: cols_out(to, kind).wait_send())
        for k in range(2):
            cols_on(kind, k).wait_send()
    pair_out(0).wait_send()
    pair_out(1).wait_send()
    for stage in stages:
        each_group(lambda i, stage=stage: grads_out(i, *stage).wait_send())
        each_group(lambda i, stage=stage: grads_in(i, *stage).wait_recv())
        kinds = slice(stage[0], stage[0] + stage[1])
        for c in range(chips):
            acc = gr[c * reps, kinds].astype(F32)
            for r in range(1, reps):
                acc = acc + gr[c * reps + r, kinds].astype(F32)
            grads[kinds, :, c * 2 * hd : (c + 1) * 2 * hd] = acc


def by_heads(n, reps, tokens, cotangent, weights, neighbour_lists, neighbour_counts):
    width = tokens.shape[2]
    slab = n * BLOCK
    cols = weights.shape[2]
    part = width // (n * reps)
    groups = (n // 2) * reps
    vmem = pl.BlockSpec(memory_space=pltpu.VMEM)
    hbm = pl.BlockSpec(memory_space=pl.ANY)
    dma = pltpu.SemaphoreType.DMA
    return pl.pallas_call(
        functools.partial(layer_kernel, n, reps),
        out_shape=(
            jax.ShapeDtypeStruct(tokens.shape, BF16),
            jax.ShapeDtypeStruct(tokens.shape, BF16),
            jax.ShapeDtypeStruct((4, part, cols), F32),
        ),
        in_specs=[hbm] * 3 + [vmem] * 2,
        out_specs=(vmem, vmem, vmem),
        scratch_shapes=[
            pltpu.VMEM((BLOCK, width), BF16),
            pltpu.VMEM((BLOCK, width), BF16),
            pltpu.VMEM(weights.shape, BF16),
            pltpu.VMEM((n, 2, BLOCK, 2 * HEAD_DIM), BF16),
            pltpu.VMEM((n, 2, BLOCK, 2 * HEAD_DIM), BF16),
            pltpu.VMEM((2, 2, BLOCK, width // 2), BF16),
            pltpu.VMEM((n, 2, BLOCK, width // 2), BF16),
            pltpu.VMEM((HEAD_DIM, slab), BF16),
            pltpu.VMEM((HEAD_DIM, slab), BF16),
            pltpu.VMEM((HEAD_DIM, slab), BF16),
            pltpu.VMEM((HEAD_DIM, slab), BF16),
            pltpu.VMEM((slab, HEAD_DIM), BF16),
            pltpu.VMEM((slab, HEAD_DIM), BF16),
            pltpu.VMEM((HEAD_DIM, slab), F32),
            pltpu.VMEM((HEAD_DIM, slab), F32),
            pltpu.VMEM((n, slab), F32),
            pltpu.VMEM((slab, slab), F32),
            pltpu.VMEM((slab, HEAD_DIM), BF16),
            pltpu.VMEM((slab, HEAD_DIM), BF16),
            pltpu.VMEM((2, 2, 2 * HEAD_DIM, slab), BF16),
            pltpu.VMEM((2, slab, 2 * HEAD_DIM), BF16),
            pltpu.VMEM((n, 2, BLOCK, 2 * HEAD_DIM), BF16),
            pltpu.VMEM((groups, 4, part, 2 * HEAD_DIM), BF16),
            pltpu.VMEM((groups, 4, part, 2 * HEAD_DIM), BF16),
            dma((6,)),
            dma((2, n)), dma((2, n)), dma((2, n)), dma((2, n)), dma((2, 2)),
            dma((2, n)), dma((2, n)),
            dma((2,)), dma((2,)), dma((3, groups)), dma((3, groups)),
        ],
        compiler_params=pltpu.CompilerParams(
            collective_id=0, has_side_effects=True, vmem_limit_bytes=53 * 1024 * 1024
        ),
        cost_estimate=pl.CostEstimate(
            flops=3 * 10**9, bytes_accessed=6 * 2**20, transcendentals=2**20
        ),
    )(tokens, cotangent, weights, neighbour_lists, neighbour_counts)


def split_heads(matrix):
    return matrix.reshape(matrix.shape[:-1] + (HEADS, HEAD_DIM))


def body(tokens, cotangent, weights, neighbour_lists, neighbour_counts):
    score_scale = 1.0 / math.sqrt(HEAD_DIM)
    inputs = tokens[0]
    upstream = cotangent[0]
    row_count = inputs.shape[0]
    local_blocks = row_count // BLOCK
    w_query, w_key, w_value, w_out = (weights[0], weights[1], weights[2], weights[3])
    queries = (
        jnp.dot(inputs, w_query, preferred_element_type=jnp.float32)
        .astype(jnp.bfloat16)
        .reshape(local_blocks, BLOCK, -1)
    )
    key_rows = (
        jnp.dot(inputs, w_key, preferred_element_type=jnp.float32)
        .astype(jnp.bfloat16)
        .reshape(local_blocks, BLOCK, -1)
    )
    value_rows = (
        jnp.dot(inputs, w_value, preferred_element_type=jnp.float32)
        .astype(jnp.bfloat16)
        .reshape(local_blocks, BLOCK, -1)
    )
    all_keys, all_values = (
        lax.all_gather(key_rows, "seq", axis=0, tiled=True),
        lax.all_gather(value_rows, "seq", axis=0, tiled=True),
    )
    slab_blocks = all_keys.shape[0]
    first_block = lax.axis_index("seq") * local_blocks
    lists_all = neighbour_lists[0]
    counts_all = neighbour_counts[0]
    my_lists = lax.dynamic_slice_in_dim(lists_all, first_block, local_blocks, 0)
    my_counts = lax.dynamic_slice_in_dim(counts_all, first_block, local_blocks, 0)
    slot_keys = split_heads(
        jnp.take(all_keys, my_lists, axis=0).reshape(local_blocks, MAXN * BLOCK, -1)
    )
    slot_values = split_heads(
        jnp.take(all_values, my_lists, axis=0).reshape(local_blocks, MAXN * BLOCK, -1)
    )
    query_heads = split_heads(queries)
    scores = (
        jnp.einsum("bqhd,bkhd->bhqk", query_heads, slot_keys, preferred_element_type=jnp.float32)
        * score_scale
    )
    live_cols = (jnp.arange(MAXN * BLOCK) // BLOCK)[None, :] < my_counts[:, None]
    scores = jnp.where(live_cols[:, None, None, :], scores, -1e30)
    row_max = jnp.max(scores, axis=-1)
    exponent = jnp.exp(scores - row_max[..., None])
    totals = jnp.sum(exponent, axis=-1)
    mixed = jnp.einsum(
        "bhqk,bkhd->bqhd",
        exponent.astype(jnp.bfloat16),
        slot_values,
        preferred_element_type=jnp.float32,
    )
    attended = (
        (mixed / jnp.transpose(totals, (0, 2, 1))[..., None])
        .astype(jnp.bfloat16)
        .reshape(row_count, -1)
    )
    output = lax.dot_general(
        attended, w_out, (((1,), (1,)), ((), ())), preferred_element_type=jnp.float32
    ).astype(jnp.bfloat16)
    d_attended = jnp.dot(upstream, w_out, preferred_element_type=jnp.float32).astype(jnp.bfloat16)
    grad_out = lax.dot_general(
        upstream, attended, (((0,), (0,)), ((), ())), preferred_element_type=jnp.float32
    )
    d_blocks = d_attended.reshape(local_blocks, BLOCK, -1)
    d_heads = split_heads(d_blocks)
    attended_heads = split_heads(attended.reshape(local_blocks, BLOCK, -1))
    row_delta = jnp.transpose(
        jnp.sum(d_heads.astype(jnp.float32) * attended_heads.astype(jnp.float32), axis=-1),
        (0, 2, 1),
    )
    normed = exponent / totals[..., None]
    d_probs = jnp.einsum(
        "bqhd,bkhd->bhqk", d_heads, slot_values, preferred_element_type=jnp.float32
    )
    d_scores = (normed * (d_probs - row_delta[..., None])).astype(jnp.bfloat16)
    d_queries = (
        (
            jnp.einsum("bhqk,bkhd->bqhd", d_scores, slot_keys, preferred_element_type=jnp.float32)
            * score_scale
        )
        .astype(jnp.bfloat16)
        .reshape(row_count, -1)
    )
    gathered_query, gathered_dattn = (
        lax.all_gather(queries, "seq", axis=0, tiled=True),
        lax.all_gather(d_blocks, "seq", axis=0, tiled=True),
    )
    gathered_max, gathered_total, gathered_delta = (
        lax.all_gather(row_max, "seq", axis=0, tiled=True),
        lax.all_gather(totals, "seq", axis=0, tiled=True),
        lax.all_gather(row_delta, "seq", axis=0, tiled=True),
    )
    owners = first_block + jnp.arange(local_blocks)
    live_slots = jnp.arange(MAXN)[None, :] < counts_all[:, None]
    listed = jnp.any(
        (lists_all[:, :, None] == owners[None, None, :]) & live_slots[:, :, None], axis=1
    )
    groups = slab_blocks // 8
    own_keys = split_heads(key_rows)
    own_values = split_heads(value_rows)

    def regroup(matrix):
        return matrix.reshape((groups, 8) + matrix.shape[1:])

    def accumulate(carry, group_data):
        group_query, group_dattn, group_max, group_total, group_delta, group_listed = group_data
        group_query = split_heads(group_query)
        group_dattn = split_heads(group_dattn)
        group_scores = (
            jnp.einsum(
                "cqhd,ikhd->cihqk", group_query, own_keys, preferred_element_type=jnp.float32
            )
            * score_scale
        )
        group_scores = jnp.where(group_listed[:, :, None, None, None], group_scores, -1e30)
        group_probs = (
            jnp.exp(group_scores - group_max[:, None, :, :, None])
            / group_total[:, None, :, :, None]
        )
        group_dprobs = jnp.einsum(
            "cqhd,ikhd->cihqk", group_dattn, own_values, preferred_element_type=jnp.float32
        )
        group_dscores = (group_probs * (group_dprobs - group_delta[:, None, :, :, None])).astype(
            jnp.bfloat16
        )
        key_next = carry[0] + jnp.einsum(
            "cihqk,cqhd->ikhd", group_dscores, group_query, preferred_element_type=jnp.float32
        )
        value_next = carry[1] + jnp.einsum(
            "cihqk,cqhd->ikhd",
            group_probs.astype(jnp.bfloat16),
            group_dattn,
            preferred_element_type=jnp.float32,
        )
        return ((key_next, value_next), None)

    zero_sum = jnp.zeros((local_blocks, BLOCK, HEADS, HEAD_DIM), jnp.float32)
    group_inputs = (
        regroup(gathered_query),
        regroup(gathered_dattn),
        regroup(gathered_max),
        regroup(gathered_total),
        regroup(gathered_delta),
        regroup(listed),
    )
    (key_heads, value_heads), _ = lax.scan(accumulate, (zero_sum, zero_sum), group_inputs)
    key_sum = (key_heads * score_scale).reshape(local_blocks, BLOCK, -1)
    value_sum = value_heads.reshape(local_blocks, BLOCK, -1)
    d_keys = key_sum.astype(jnp.bfloat16).reshape(row_count, -1)
    d_values = value_sum.astype(jnp.bfloat16).reshape(row_count, -1)
    stacked = jnp.concatenate([d_queries, d_keys, d_values], axis=1)
    w_joined = jnp.concatenate([w_query, w_key, w_value], axis=1)
    d_inputs = lax.dot_general(
        stacked, w_joined, (((1,), (1,)), ((), ())), preferred_element_type=jnp.float32
    ).astype(jnp.bfloat16)
    grad_joined = lax.dot_general(
        inputs, stacked, (((0,), (0,)), ((), ())), preferred_element_type=jnp.float32
    )
    width_model = inputs.shape[1]
    grad_three = jnp.transpose(grad_joined.reshape(width_model, 3, -1), (1, 0, 2))
    grads = jnp.concatenate([grad_three, grad_out[None]], axis=0)
    within_slab = lax.psum_scatter(
        grads.astype(jnp.bfloat16), "seq", scatter_dimension=1, tiled=True
    )
    summed = lax.psum_scatter(within_slab, "rep", scatter_dimension=1, tiled=True).astype(
        jnp.float32
    )
    return (output[None], d_inputs[None], summed)


def solution(mesh):
    placed = (
        P("rep", "seq", None),
        P("rep", "seq", None),
        P(),
        P("rep", None, None),
        P("rep", None),
    )
    n, reps = mesh.shape["seq"], mesh.shape["rep"]
    run = functools.partial(by_heads, n, reps) if n == HEADS else body
    return jax.shard_map(
        run,
        mesh=mesh,
        in_specs=placed,
        out_specs=(P("rep", "seq", None), P("rep", "seq", None), P(None, ("seq", "rep"), None)),
        check_vma=False,
    )
```

```python
import functools
import math

import jax
import jax.numpy as jnp
from jax import lax
from jax.experimental import pallas as pl
from jax.experimental.pallas import tpu as pltpu
from jax.sharding import PartitionSpec as P

HEADS = 8
HEAD_DIM = 64
BLOCK = 128
MAXN = 27


F32 = jnp.float32
BF16 = jnp.bfloat16


def mm(a, b):
    return jnp.dot(a, b, preferred_element_type=F32)


def mm_nt(a, b):
    return lax.dot_general(a, b, (((1,), (1,)), ((), ())), preferred_element_type=F32)


def layer_kernel(
    n, reps,
    tok_hbm, cot_hbm, w_hbm, lists, counts,
    out, dinp, grads,
    tok, cot, w, send1, recv1, tstage, trecv, kt, vt, qtr, dtr, kx, vx, dkt, dvt, bias,
    normed_all, e_all, total_all, att_all, dq_all, xp, bk, back, gs, gr,
    ls, ss1, rs1, sst, rst, srl, ssb, rsb, ssp, rsp, ssg, rsg,
):
    me = lax.axis_index("seq")
    rep = lax.axis_index("rep")
    core = lax.rem(me, 2)
    chip = me // 2
    chips = n // 2
    scale = 1.0 / math.sqrt(HEAD_DIM)
    hd = HEAD_DIM
    part = gs.shape[2]

    loads = [
        pltpu.make_async_copy(tok_hbm.at[0], tok, ls.at[0]),
        pltpu.make_async_copy(cot_hbm.at[0], cot, ls.at[1]),
    ] + [pltpu.make_async_copy(w_hbm.at[j], w.at[j], ls.at[2 + j]) for j in range(4)]
    for load in loads:
        load.start()

    def remote(src, dst, s_sem, r_sem, seq, z):
        return pltpu.make_async_remote_copy(
            src_ref=src, dst_ref=dst, send_sem=s_sem, recv_sem=r_sem,
            device_id={"seq": seq, "rep": z}, device_id_type=pl.DeviceIdType.MESH,
        )

    barrier = pltpu.get_barrier_semaphore()

    def greet_seq(i, carry):
        pl.semaphore_signal(
            barrier, inc=1, device_id={"seq": lax.rem(me + i, n), "rep": rep},
            device_id_type=pl.DeviceIdType.MESH,
        )
        return carry

    def greet_rep(i, carry):
        pl.semaphore_signal(
            barrier, inc=1,
            device_id={
                "seq": lax.rem(me + 2 * lax.rem(i, chips), n),
                "rep": lax.rem(rep + 1 + i // chips, reps),
            },
            device_id_type=pl.DeviceIdType.MESH,
        )
        return carry

    lax.fori_loop(1, n, greet_seq, 0)
    lax.fori_loop(0, (reps - 1) * chips, greet_rep, 0)

    def each_peer(act):
        def step(i, carry):
            act(lax.rem(me + i, n))
            return carry

        lax.fori_loop(1, n, step, 0)

    x_chip = chip + 1 - 2 * lax.rem(chip, 2)
    y_chip = chip + 2 - 4 * (chip // 2)
    far_chip = chips - 1 - chip
    other = me + 1 - 2 * core

    def stage_cols(kind, ref):
        for s in range(n):
            cols = slice((s // 2) * BLOCK, (s // 2 + 1) * BLOCK)
            tstage[s % 2, kind, :, cols] = ref[:, s * BLOCK : (s + 1) * BLOCK]

    def cols_out(to, kind):
        return remote(
            tstage.at[lax.rem(to, 2), kind], trecv.at[me, kind],
            sst.at[kind, to], rst.at[kind, me], to, rep,
        )

    def cols_in(src, kind):
        return remote(
            tstage.at[core, kind], trecv.at[src, kind],
            sst.at[kind, src], rst.at[kind, src], src, rep,
        )

    def cols_on(kind, k):
        src, to = (y_chip, x_chip) if kind == 0 else (x_chip, y_chip)
        block = 2 * src + k
        return remote(
            trecv.at[block, kind], trecv.at[block, kind],
            srl.at[kind, k], rst.at[kind, block], 2 * to + core, rep,
        )

    def near(kind, act):
        act(other, kind)
        for k in range(2):
            act(2 * x_chip + k, kind)
            act(2 * y_chip + k, kind)

    def forward_cols(kind):
        for k in range(2):
            cols_in(2 * (y_chip if kind == 0 else x_chip) + k, kind).wait_recv()
            cols_on(kind, k).start()

    def finish_cols(kind):
        cols_in(other, kind).wait_recv()
        for k in range(2):
            cols_in(2 * (x_chip if kind == 0 else y_chip) + k, kind).wait_recv()
            cols_in(2 * far_chip + k, kind).wait_recv()

    loads[0].wait()
    stage_cols(0, tok)
    pl.semaphore_wait(barrier, n - 1 + (reps - 1) * chips)
    near(0, lambda to, kind: cols_out(to, kind).start())
    loads[1].wait()
    stage_cols(1, cot)

    def heads_out(to, piece):
        return remote(
            send1.at[to, piece], recv1.at[me, piece],
            ss1.at[piece, to], rs1.at[piece, me], to, rep,
        )

    def heads_in(src, piece):
        return remote(
            send1.at[src, piece], recv1.at[src, piece],
            ss1.at[piece, src], rs1.at[piece, src], src, rep,
        )

    def pack(piece, one, two):
        for h in range(n):
            cols = slice(h * hd, (h + 1) * hd)
            send1[h, piece] = jnp.concatenate([one[:, cols], two[:, cols]], axis=1)
        each_peer(lambda to: heads_out(to, piece).start())
        recv1[me, piece] = send1[me, piece]

    x = tok[...]
    loads[2].wait()
    q = (mm(x, w[0]).astype(BF16).astype(F32) * scale).astype(BF16)
    loads[3].wait()
    k = mm(x, w[1]).astype(BF16)
    pack(0, q, k)
    loads[4].wait()
    v = mm(x, w[2]).astype(BF16)
    loads[5].wait()
    da = mm(cot[...], w[3]).astype(BF16)
    pack(1, v, da)
    near(1, lambda to, kind: cols_out(to, kind).start())

    trecv[pl.ds(me, 1)] = tstage[pl.ds(core, 1)]

    eye = lax.broadcasted_iota(jnp.int32, (n, n), 0) == lax.broadcasted_iota(jnp.int32, (n, n), 1)
    count_col = jnp.sum(
        jnp.where(eye, jnp.broadcast_to(counts[...].astype(F32), (n, n)), 0.0),
        axis=1, keepdims=True,
    )
    listed = lists[0]
    slot = lax.broadcasted_iota(jnp.int32, listed.shape, 1).astype(F32)
    alive = slot < count_col
    for c in range(n):
        hit = jnp.max(
            jnp.where(jnp.logical_and(listed == c, alive), 1.0, 0.0), axis=1, keepdims=True
        )
        bias[:, c * BLOCK : (c + 1) * BLOCK] = jnp.broadcast_to((hit - 1.0) * 1e30, (n, BLOCK))
    dkt[...] = jnp.zeros_like(dkt)
    dvt[...] = jnp.zeros_like(dvt)

    each_peer(lambda src: heads_in(src, 0).wait_recv())
    for b in range(n):
        rows = slice(b * BLOCK, (b + 1) * BLOCK)
        qk = recv1[b, 0]
        kx[rows] = qk[:, hd:]
        qkt = qk.T
        qtr[:, rows] = qkt[:hd]
        kt[:, rows] = qkt[hd:]

    def back_out(b, piece):
        rows = pl.ds(pl.multiple_of(b * BLOCK, BLOCK), BLOCK)
        return remote(
            bk.at[piece, rows], back.at[me, piece],
            ssb.at[piece, b], rsb.at[piece, me], b, rep,
        )

    def back_in(h, piece):
        return remote(
            bk.at[piece, pl.ds(0, BLOCK)], back.at[h, piece],
            ssb.at[piece, h], rsb.at[piece, h], h, rep,
        )

    def pair_out(piece):
        return remote(
            xp.at[core, piece], xp.at[core, piece], ssp.at[piece], rsp.at[piece], other, rep
        )

    def pair_in(piece):
        return remote(
            xp.at[1 - core, piece], xp.at[1 - core, piece],
            ssp.at[piece], rsp.at[piece], other, rep,
        )

    def pair_of(i):
        return pl.ds(pl.multiple_of(2 * i * BLOCK, 2 * BLOCK), 2 * BLOCK)

    def two_blocks(i, piece):
        return recv1[pl.ds(2 * i, 2), piece].reshape(2 * BLOCK, 2 * hd)

    def weigh(i, carry):
        rows = pair_of(i)
        mask = [
            jnp.broadcast_to(bias[pl.ds(2 * i + j, 1), :], (BLOCK, n * BLOCK)) for j in range(2)
        ]
        s = mm(two_blocks(i, 0)[:, :hd], kt[...]) + jnp.concatenate(mask, axis=0)
        e = jnp.exp(s - jnp.max(s, axis=1, keepdims=True))
        total = jnp.sum(e, axis=1, keepdims=True)
        e_all[rows] = e.astype(BF16)
        total_all[rows] = total
        normed_all[rows] = e * (1.0 / total)
        return carry

    def forward(i, carry):
        rows = pair_of(i)
        att = (mm(e_all[rows], vx[...]) / total_all[rows]).astype(BF16)
        att_all[rows] = att
        xp[core, 0, :hd, rows] = att.T
        dvt[...] += mm(dtr[:, rows], normed_all[rows].astype(BF16))
        return carry

    forward_cols(0)
    lax.fori_loop(0, n // 2, weigh, 0, unroll=2)
    each_peer(lambda src: heads_in(src, 1).wait_recv())
    for b in range(n):
        rows = slice(b * BLOCK, (b + 1) * BLOCK)
        vd = recv1[b, 1]
        vx[rows] = vd[:, :hd]
        vdt = vd.T
        vt[:, rows] = vdt[:hd]
        dtr[:, rows] = vdt[hd:]

    lax.fori_loop(0, n // 2, forward, 0, unroll=2)
    xp[core, 0, hd:] = dvt[...].astype(BF16)
    pair_out(0).start()

    for b in range(n):
        rows = slice(b * BLOCK, (b + 1) * BLOCK)
        bk[0, rows] = jnp.concatenate([att_all[rows], dvt[:, rows].T.astype(BF16)], axis=1)
    each_peer(lambda to: back_out(to, 0).start())

    def backward(i, carry):
        rows = pair_of(i)
        dab = two_blocks(i, 1)[:, hd:]
        delta = jnp.sum(dab.astype(F32) * att_all[rows].astype(F32), axis=1, keepdims=True)
        ds = (normed_all[rows] * (mm(dab, vt[...]) - delta)).astype(BF16)
        dkt[...] += mm(qtr[:, rows], ds)
        dq = (mm(ds, kx[...]) * scale).astype(BF16)
        dq_all[rows] = dq
        xp[core, 1, :hd, rows] = dq.T
        return carry

    def grads_out(i, k0, count, stage):
        chip_to = lax.rem(chip + i, chips)
        rep_to = lax.rem(rep + i // chips, reps)
        to = chip_to * reps + rep_to
        here = chip * reps + rep
        return remote(
            gs.at[to, pl.ds(k0, count)], gr.at[here, pl.ds(k0, count)],
            ssg.at[stage, to], rsg.at[stage, here], 2 * chip_to + core, rep_to,
        )

    def grads_in(i, k0, count, stage):
        chip_from = lax.rem(chip + i, chips)
        rep_from = lax.rem(rep + i // chips, reps)
        src = chip_from * reps + rep_from
        return remote(
            gs.at[src, pl.ds(k0, count)], gr.at[src, pl.ds(k0, count)],
            ssg.at[stage, src], rsg.at[stage, src], 2 * chip_from + core, rep_from,
        )

    stages = ((2, 1, 0), (3, 1, 1), (0, 2, 2))

    def each_group(act):
        def step(i, carry):
            act(i)
            return carry

        lax.fori_loop(1, chips * reps, step, 0)

    def product(kinds, column_kind, piece, rows):
        left = jnp.concatenate(
            [xp[c, piece][r] for r in rows for c in range(2)], axis=0
        )
        right = trecv[:, column_kind].reshape(n * BLOCK, trecv.shape[3])
        total = mm(left, right).astype(BF16)
        for j, kind in enumerate(kinds):
            one = total[2 * hd * j : 2 * hd * (j + 1)].T
            gs[:, kind] = one.reshape(chips * reps, part, 2 * hd)

    low, high = slice(0, hd), slice(hd, 2 * hd)
    lax.fori_loop(0, 2, backward, 0, unroll=2)
    forward_cols(1)
    finish_cols(0)
    pair_in(0).wait_recv()
    product((2,), 0, 0, (high,))
    each_group(lambda i: grads_out(i, *stages[0]).start())
    lax.fori_loop(2, n // 2, backward, 0, unroll=2)

    xp[core, 1, hd:] = dkt[...].astype(BF16)
    pair_out(1).start()
    finish_cols(1)
    product((3,), 1, 0, (low,))
    each_group(lambda i: grads_out(i, *stages[1]).start())
    pair_in(1).wait_recv()
    product((0, 1), 0, 1, (low, high))
    each_group(lambda i: grads_out(i, *stages[2]).start())
    gr[pl.ds(chip * reps + rep, 1)] = gs[pl.ds(chip * reps + rep, 1)]

    for b in range(n):
        rows = slice(b * BLOCK, (b + 1) * BLOCK)
        bk[1, rows] = jnp.concatenate([dq_all[rows], dkt[:, rows].T.astype(BF16)], axis=1)
    each_peer(lambda to: back_out(to, 1).start())
    mine = pl.ds(pl.multiple_of(me * BLOCK, BLOCK), BLOCK)
    for piece in range(2):
        back[me, piece] = bk[piece, mine]

    each_peer(lambda src: back_in(src, 0).wait_recv())
    att = jnp.concatenate([back[h, 0][:, :hd] for h in range(n)], axis=1)
    dv = jnp.concatenate([back[h, 0][:, hd:] for h in range(n)], axis=1)
    out[0] = mm_nt(att, w[3]).astype(BF16)
    each_peer(lambda src: back_in(src, 1).wait_recv())
    dq = jnp.concatenate([back[h, 1][:, :hd] for h in range(n)], axis=1)
    dk = jnp.concatenate([back[h, 1][:, hd:] for h in range(n)], axis=1)
    dinp[0] = (mm_nt(dq, w[0]) + mm_nt(dk, w[1]) + mm_nt(dv, w[2])).astype(BF16)

    def drain(to):
        for piece in range(2):
            heads_out(to, piece).wait_send()
            back_out(to, piece).wait_send()

    each_peer(drain)
    for kind in range(2):
        near(kind, lambda to, kind: cols_out(to, kind).wait_send())
        for k in range(2):
            cols_on(kind, k).wait_send()
    pair_out(0).wait_send()
    pair_out(1).wait_send()
    for stage in stages:
        each_group(lambda i, stage=stage: grads_out(i, *stage).wait_send())
        each_group(lambda i, stage=stage: grads_in(i, *stage).wait_recv())
        kinds = slice(stage[0], stage[0] + stage[1])
        for c in range(chips):
            acc = gr[c * reps, kinds].astype(F32)
            for r in range(1, reps):
                acc = acc + gr[c * reps + r, kinds].astype(F32)
            grads[kinds, :, c * 2 * hd : (c + 1) * 2 * hd] = acc


def by_heads(n, reps, tokens, cotangent, weights, neighbour_lists, neighbour_counts):
    width = tokens.shape[2]
    slab = n * BLOCK
    cols = weights.shape[2]
    part = width // (n * reps)
    groups = (n // 2) * reps
    vmem = pl.BlockSpec(memory_space=pltpu.VMEM)
    hbm = pl.BlockSpec(memory_space=pl.ANY)
    dma = pltpu.SemaphoreType.DMA
    return pl.pallas_call(
        functools.partial(layer_kernel, n, reps),
        out_shape=(
            jax.ShapeDtypeStruct(tokens.shape, BF16),
            jax.ShapeDtypeStruct(tokens.shape, BF16),
            jax.ShapeDtypeStruct((4, part, cols), F32),
        ),
        in_specs=[hbm] * 3 + [vmem] * 2,
        out_specs=(vmem, vmem, vmem),
        scratch_shapes=[
            pltpu.VMEM((BLOCK, width), BF16),
            pltpu.VMEM((BLOCK, width), BF16),
            pltpu.VMEM(weights.shape, BF16),
            pltpu.VMEM((n, 2, BLOCK, 2 * HEAD_DIM), BF16),
            pltpu.VMEM((n, 2, BLOCK, 2 * HEAD_DIM), BF16),
            pltpu.VMEM((2, 2, BLOCK, width // 2), BF16),
            pltpu.VMEM((n, 2, BLOCK, width // 2), BF16),
            pltpu.VMEM((HEAD_DIM, slab), BF16),
            pltpu.VMEM((HEAD_DIM, slab), BF16),
            pltpu.VMEM((HEAD_DIM, slab), BF16),
            pltpu.VMEM((HEAD_DIM, slab), BF16),
            pltpu.VMEM((slab, HEAD_DIM), BF16),
            pltpu.VMEM((slab, HEAD_DIM), BF16),
            pltpu.VMEM((HEAD_DIM, slab), F32),
            pltpu.VMEM((HEAD_DIM, slab), F32),
            pltpu.VMEM((n, slab), F32),
            pltpu.VMEM((slab, slab), F32),
            pltpu.VMEM((slab, slab), BF16),
            pltpu.VMEM((slab, 1), F32),
            pltpu.VMEM((slab, HEAD_DIM), BF16),
            pltpu.VMEM((slab, HEAD_DIM), BF16),
            pltpu.VMEM((2, 2, 2 * HEAD_DIM, slab), BF16),
            pltpu.VMEM((2, slab, 2 * HEAD_DIM), BF16),
            pltpu.VMEM((n, 2, BLOCK, 2 * HEAD_DIM), BF16),
            pltpu.VMEM((groups, 4, part, 2 * HEAD_DIM), BF16),
            pltpu.VMEM((groups, 4, part, 2 * HEAD_DIM), BF16),
            dma((6,)),
            dma((2, n)), dma((2, n)), dma((2, n)), dma((2, n)), dma((2, 2)),
            dma((2, n)), dma((2, n)),
            dma((2,)), dma((2,)), dma((3, groups)), dma((3, groups)),
        ],
        compiler_params=pltpu.CompilerParams(
            collective_id=0, has_side_effects=True, vmem_limit_bytes=53 * 1024 * 1024
        ),
        cost_estimate=pl.CostEstimate(
            flops=3 * 10**9, bytes_accessed=6 * 2**20, transcendentals=2**20
        ),
    )(tokens, cotangent, weights, neighbour_lists, neighbour_counts)


def split_heads(matrix):
    return matrix.reshape(matrix.shape[:-1] + (HEADS, HEAD_DIM))


def body(tokens, cotangent, weights, neighbour_lists, neighbour_counts):
    score_scale = 1.0 / math.sqrt(HEAD_DIM)
    inputs = tokens[0]
    upstream = cotangent[0]
    row_count = inputs.shape[0]
    local_blocks = row_count // BLOCK
    w_query, w_key, w_value, w_out = (weights[0], weights[1], weights[2], weights[3])
    queries = (
        jnp.dot(inputs, w_query, preferred_element_type=jnp.float32)
        .astype(jnp.bfloat16)
        .reshape(local_blocks, BLOCK, -1)
    )
    key_rows = (
        jnp.dot(inputs, w_key, preferred_element_type=jnp.float32)
        .astype(jnp.bfloat16)
        .reshape(local_blocks, BLOCK, -1)
    )
    value_rows = (
        jnp.dot(inputs, w_value, preferred_element_type=jnp.float32)
        .astype(jnp.bfloat16)
        .reshape(local_blocks, BLOCK, -1)
    )
    all_keys, all_values = (
        lax.all_gather(key_rows, "seq", axis=0, tiled=True),
        lax.all_gather(value_rows, "seq", axis=0, tiled=True),
    )
    slab_blocks = all_keys.shape[0]
    first_block = lax.axis_index("seq") * local_blocks
    lists_all = neighbour_lists[0]
    counts_all = neighbour_counts[0]
    my_lists = lax.dynamic_slice_in_dim(lists_all, first_block, local_blocks, 0)
    my_counts = lax.dynamic_slice_in_dim(counts_all, first_block, local_blocks, 0)
    slot_keys = split_heads(
        jnp.take(all_keys, my_lists, axis=0).reshape(local_blocks, MAXN * BLOCK, -1)
    )
    slot_values = split_heads(
        jnp.take(all_values, my_lists, axis=0).reshape(local_blocks, MAXN * BLOCK, -1)
    )
    query_heads = split_heads(queries)
    scores = (
        jnp.einsum("bqhd,bkhd->bhqk", query_heads, slot_keys, preferred_element_type=jnp.float32)
        * score_scale
    )
    live_cols = (jnp.arange(MAXN * BLOCK) // BLOCK)[None, :] < my_counts[:, None]
    scores = jnp.where(live_cols[:, None, None, :], scores, -1e30)
    row_max = jnp.max(scores, axis=-1)
    exponent = jnp.exp(scores - row_max[..., None])
    totals = jnp.sum(exponent, axis=-1)
    mixed = jnp.einsum(
        "bhqk,bkhd->bqhd",
        exponent.astype(jnp.bfloat16),
        slot_values,
        preferred_element_type=jnp.float32,
    )
    attended = (
        (mixed / jnp.transpose(totals, (0, 2, 1))[..., None])
        .astype(jnp.bfloat16)
        .reshape(row_count, -1)
    )
    output = lax.dot_general(
        attended, w_out, (((1,), (1,)), ((), ())), preferred_element_type=jnp.float32
    ).astype(jnp.bfloat16)
    d_attended = jnp.dot(upstream, w_out, preferred_element_type=jnp.float32).astype(jnp.bfloat16)
    grad_out = lax.dot_general(
        upstream, attended, (((0,), (0,)), ((), ())), preferred_element_type=jnp.float32
    )
    d_blocks = d_attended.reshape(local_blocks, BLOCK, -1)
    d_heads = split_heads(d_blocks)
    attended_heads = split_heads(attended.reshape(local_blocks, BLOCK, -1))
    row_delta = jnp.transpose(
        jnp.sum(d_heads.astype(jnp.float32) * attended_heads.astype(jnp.float32), axis=-1),
        (0, 2, 1),
    )
    normed = exponent / totals[..., None]
    d_probs = jnp.einsum(
        "bqhd,bkhd->bhqk", d_heads, slot_values, preferred_element_type=jnp.float32
    )
    d_scores = (normed * (d_probs - row_delta[..., None])).astype(jnp.bfloat16)
    d_queries = (
        (
            jnp.einsum("bhqk,bkhd->bqhd", d_scores, slot_keys, preferred_element_type=jnp.float32)
            * score_scale
        )
        .astype(jnp.bfloat16)
        .reshape(row_count, -1)
    )
    gathered_query, gathered_dattn = (
        lax.all_gather(queries, "seq", axis=0, tiled=True),
        lax.all_gather(d_blocks, "seq", axis=0, tiled=True),
    )
    gathered_max, gathered_total, gathered_delta = (
        lax.all_gather(row_max, "seq", axis=0, tiled=True),
        lax.all_gather(totals, "seq", axis=0, tiled=True),
        lax.all_gather(row_delta, "seq", axis=0, tiled=True),
    )
    owners = first_block + jnp.arange(local_blocks)
    live_slots = jnp.arange(MAXN)[None, :] < counts_all[:, None]
    listed = jnp.any(
        (lists_all[:, :, None] == owners[None, None, :]) & live_slots[:, :, None], axis=1
    )
    groups = slab_blocks // 8
    own_keys = split_heads(key_rows)
    own_values = split_heads(value_rows)

    def regroup(matrix):
        return matrix.reshape((groups, 8) + matrix.shape[1:])

    def accumulate(carry, group_data):
        group_query, group_dattn, group_max, group_total, group_delta, group_listed = group_data
        group_query = split_heads(group_query)
        group_dattn = split_heads(group_dattn)
        group_scores = (
            jnp.einsum(
                "cqhd,ikhd->cihqk", group_query, own_keys, preferred_element_type=jnp.float32
            )
            * score_scale
        )
        group_scores = jnp.where(group_listed[:, :, None, None, None], group_scores, -1e30)
        group_probs = (
            jnp.exp(group_scores - group_max[:, None, :, :, None])
            / group_total[:, None, :, :, None]
        )
        group_dprobs = jnp.einsum(
            "cqhd,ikhd->cihqk", group_dattn, own_values, preferred_element_type=jnp.float32
        )
        group_dscores = (group_probs * (group_dprobs - group_delta[:, None, :, :, None])).astype(
            jnp.bfloat16
        )
        key_next = carry[0] + jnp.einsum(
            "cihqk,cqhd->ikhd", group_dscores, group_query, preferred_element_type=jnp.float32
        )
        value_next = carry[1] + jnp.einsum(
            "cihqk,cqhd->ikhd",
            group_probs.astype(jnp.bfloat16),
            group_dattn,
            preferred_element_type=jnp.float32,
        )
        return ((key_next, value_next), None)

    zero_sum = jnp.zeros((local_blocks, BLOCK, HEADS, HEAD_DIM), jnp.float32)
    group_inputs = (
        regroup(gathered_query),
        regroup(gathered_dattn),
        regroup(gathered_max),
        regroup(gathered_total),
        regroup(gathered_delta),
        regroup(listed),
    )
    (key_heads, value_heads), _ = lax.scan(accumulate, (zero_sum, zero_sum), group_inputs)
    key_sum = (key_heads * score_scale).reshape(local_blocks, BLOCK, -1)
    value_sum = value_heads.reshape(local_blocks, BLOCK, -1)
    d_keys = key_sum.astype(jnp.bfloat16).reshape(row_count, -1)
    d_values = value_sum.astype(jnp.bfloat16).reshape(row_count, -1)
    stacked = jnp.concatenate([d_queries, d_keys, d_values], axis=1)
    w_joined = jnp.concatenate([w_query, w_key, w_value], axis=1)
    d_inputs = lax.dot_general(
        stacked, w_joined, (((1,), (1,)), ((), ())), preferred_element_type=jnp.float32
    ).astype(jnp.bfloat16)
    grad_joined = lax.dot_general(
        inputs, stacked, (((0,), (0,)), ((), ())), preferred_element_type=jnp.float32
    )
    width_model = inputs.shape[1]
    grad_three = jnp.transpose(grad_joined.reshape(width_model, 3, -1), (1, 0, 2))
    grads = jnp.concatenate([grad_three, grad_out[None]], axis=0)
    within_slab = lax.psum_scatter(
        grads.astype(jnp.bfloat16), "seq", scatter_dimension=1, tiled=True
    )
    summed = lax.psum_scatter(within_slab, "rep", scatter_dimension=1, tiled=True).astype(
        jnp.float32
    )
    return (output[None], d_inputs[None], summed)


def solution(mesh):
    placed = (
        P("rep", "seq", None),
        P("rep", "seq", None),
        P(),
        P("rep", None, None),
        P("rep", None),
    )
    n, reps = mesh.shape["seq"], mesh.shape["rep"]
    run = functools.partial(by_heads, n, reps) if n == HEADS else body
    return jax.shard_map(
        run,
        mesh=mesh,
        in_specs=placed,
        out_specs=(P("rep", "seq", None), P("rep", "seq", None), P(None, ("seq", "rep"), None)),
        check_vma=False,
    )
```

```python
import functools
import math

import jax
import jax.numpy as jnp
from jax import lax
from jax.experimental import pallas as pl
from jax.experimental.pallas import tpu as pltpu
from jax.sharding import PartitionSpec as P

HEADS = 8
HEAD_DIM = 64
BLOCK = 128
MAXN = 27


F32 = jnp.float32
BF16 = jnp.bfloat16


def mm(a, b):
    return jnp.dot(a, b, preferred_element_type=F32)


def mm_nt(a, b):
    return lax.dot_general(a, b, (((1,), (1,)), ((), ())), preferred_element_type=F32)


def layer_kernel(
    n, reps,
    tok_hbm, cot_hbm, w_hbm, lists, counts,
    out, dinp, grads,
    tok, cot, w, send1, recv1, tstage, trecv, kt, vt, qtr, dtr, kx, vx, dkt, dvt, bias,
    normed_all, e_all, total_all, att_all, dq_all, xp, bk, back, gs, gr,
    ls, ss1, rs1, sst, rst, srl, ssb, rsb, ssp, rsp, ssg, rsg,
):
    me = lax.axis_index("seq")
    rep = lax.axis_index("rep")
    core = lax.rem(me, 2)
    chip = me // 2
    chips = n // 2
    scale = 1.0 / math.sqrt(HEAD_DIM)
    hd = HEAD_DIM
    part = gs.shape[2]

    loads = [
        pltpu.make_async_copy(tok_hbm.at[0], tok, ls.at[0]),
        pltpu.make_async_copy(cot_hbm.at[0], cot, ls.at[1]),
    ] + [pltpu.make_async_copy(w_hbm.at[j], w.at[j], ls.at[2 + j]) for j in range(4)]
    for load in loads:
        load.start()

    def remote(src, dst, s_sem, r_sem, seq, z):
        return pltpu.make_async_remote_copy(
            src_ref=src, dst_ref=dst, send_sem=s_sem, recv_sem=r_sem,
            device_id={"seq": seq, "rep": z}, device_id_type=pl.DeviceIdType.MESH,
        )

    barrier = pltpu.get_barrier_semaphore()

    def greet_seq(i, carry):
        pl.semaphore_signal(
            barrier, inc=1, device_id={"seq": lax.rem(me + i, n), "rep": rep},
            device_id_type=pl.DeviceIdType.MESH,
        )
        return carry

    def greet_rep(i, carry):
        pl.semaphore_signal(
            barrier, inc=1,
            device_id={
                "seq": lax.rem(me + 2 * lax.rem(i, chips), n),
                "rep": lax.rem(rep + 1 + i // chips, reps),
            },
            device_id_type=pl.DeviceIdType.MESH,
        )
        return carry

    lax.fori_loop(1, n, greet_seq, 0)
    lax.fori_loop(0, (reps - 1) * chips, greet_rep, 0)

    def each_peer(act):
        def step(i, carry):
            act(lax.rem(me + i, n))
            return carry

        lax.fori_loop(1, n, step, 0)

    x_chip = chip + 1 - 2 * lax.rem(chip, 2)
    y_chip = chip + 2 - 4 * (chip // 2)
    far_chip = chips - 1 - chip
    other = me + 1 - 2 * core

    def stage_cols(kind, ref):
        for s in range(n):
            cols = slice((s // 2) * BLOCK, (s // 2 + 1) * BLOCK)
            tstage[s % 2, kind, :, cols] = ref[:, s * BLOCK : (s + 1) * BLOCK]

    def cols_out(to, kind):
        return remote(
            tstage.at[lax.rem(to, 2), kind], trecv.at[me, kind],
            sst.at[kind, to], rst.at[kind, me], to, rep,
        )

    def cols_in(src, kind):
        return remote(
            tstage.at[core, kind], trecv.at[src, kind],
            sst.at[kind, src], rst.at[kind, src], src, rep,
        )

    def cols_on(kind, k):
        src, to = (y_chip, x_chip) if kind == 0 else (x_chip, y_chip)
        block = 2 * src + k
        return remote(
            trecv.at[block, kind], trecv.at[block, kind],
            srl.at[kind, k], rst.at[kind, block], 2 * to + core, rep,
        )

    def near(kind, act):
        act(other, kind)
        for k in range(2):
            act(2 * x_chip + k, kind)
            act(2 * y_chip + k, kind)

    def forward_cols(kind):
        for k in range(2):
            cols_in(2 * (y_chip if kind == 0 else x_chip) + k, kind).wait_recv()
            cols_on(kind, k).start()

    def finish_cols(kind):
        cols_in(other, kind).wait_recv()
        for k in range(2):
            cols_in(2 * (x_chip if kind == 0 else y_chip) + k, kind).wait_recv()
            cols_in(2 * far_chip + k, kind).wait_recv()

    loads[0].wait()
    stage_cols(0, tok)
    pl.semaphore_wait(barrier, n - 1 + (reps - 1) * chips)
    near(0, lambda to, kind: cols_out(to, kind).start())
    loads[1].wait()
    stage_cols(1, cot)

    def heads_out(to, piece):
        return remote(
            send1.at[to, piece], recv1.at[me, piece],
            ss1.at[piece, to], rs1.at[piece, me], to, rep,
        )

    def heads_in(src, piece):
        return remote(
            send1.at[src, piece], recv1.at[src, piece],
            ss1.at[piece, src], rs1.at[piece, src], src, rep,
        )

    def pack(piece, one, two):
        for h in range(n):
            cols = slice(h * hd, (h + 1) * hd)
            send1[h, piece] = jnp.concatenate([one[:, cols], two[:, cols]], axis=1)
        each_peer(lambda to: heads_out(to, piece).start())
        recv1[me, piece] = send1[me, piece]

    x = tok[...]
    loads[2].wait()
    q = (mm(x, w[0]).astype(BF16).astype(F32) * scale).astype(BF16)
    loads[3].wait()
    k = mm(x, w[1]).astype(BF16)
    pack(0, q, k)
    loads[4].wait()
    v = mm(x, w[2]).astype(BF16)
    loads[5].wait()
    da = mm(cot[...], w[3]).astype(BF16)
    pack(1, v, da)
    near(1, lambda to, kind: cols_out(to, kind).start())

    trecv[pl.ds(me, 1)] = tstage[pl.ds(core, 1)]

    eye = lax.broadcasted_iota(jnp.int32, (n, n), 0) == lax.broadcasted_iota(jnp.int32, (n, n), 1)
    count_col = jnp.sum(
        jnp.where(eye, jnp.broadcast_to(counts[...].astype(F32), (n, n)), 0.0),
        axis=1, keepdims=True,
    )
    listed = lists[0]
    slot = lax.broadcasted_iota(jnp.int32, listed.shape, 1).astype(F32)
    alive = slot < count_col
    for c in range(n):
        hit = jnp.max(
            jnp.where(jnp.logical_and(listed == c, alive), 1.0, 0.0), axis=1, keepdims=True
        )
        bias[:, c * BLOCK : (c + 1) * BLOCK] = jnp.broadcast_to((hit - 1.0) * 1e30, (n, BLOCK))
    dkt[...] = jnp.zeros_like(dkt)
    dvt[...] = jnp.zeros_like(dvt)

    each_peer(lambda src: heads_in(src, 0).wait_recv())
    for b in range(n):
        rows = slice(b * BLOCK, (b + 1) * BLOCK)
        qk = recv1[b, 0]
        kx[rows] = qk[:, hd:]
        qkt = qk.T
        qtr[:, rows] = qkt[:hd]
        kt[:, rows] = qkt[hd:]

    def back_out(b, piece):
        rows = pl.ds(pl.multiple_of(b * BLOCK, BLOCK), BLOCK)
        return remote(
            bk.at[piece, rows], back.at[me, piece],
            ssb.at[piece, b], rsb.at[piece, me], b, rep,
        )

    def back_in(h, piece):
        return remote(
            bk.at[piece, pl.ds(0, BLOCK)], back.at[h, piece],
            ssb.at[piece, h], rsb.at[piece, h], h, rep,
        )

    def pair_out(piece):
        return remote(
            xp.at[core, piece], xp.at[core, piece], ssp.at[piece], rsp.at[piece], other, rep
        )

    def pair_in(piece):
        return remote(
            xp.at[1 - core, piece], xp.at[1 - core, piece],
            ssp.at[piece], rsp.at[piece], other, rep,
        )

    def pair_of(i):
        return pl.ds(pl.multiple_of(2 * i * BLOCK, 2 * BLOCK), 2 * BLOCK)

    def two_blocks(i, piece):
        return recv1[pl.ds(2 * i, 2), piece].reshape(2 * BLOCK, 2 * hd)

    def weigh(i, carry):
        rows = pair_of(i)
        mask = [
            jnp.broadcast_to(bias[pl.ds(2 * i + j, 1), :], (BLOCK, n * BLOCK)) for j in range(2)
        ]
        s = mm(two_blocks(i, 0)[:, :hd], kt[...]) + jnp.concatenate(mask, axis=0)
        e = jnp.exp(s - jnp.max(s, axis=1, keepdims=True))
        total = jnp.sum(e, axis=1, keepdims=True)
        e_all[rows] = e.astype(BF16)
        total_all[rows] = total
        normed_all[rows] = e * (1.0 / total)
        return carry

    def forward(i, carry):
        rows = pair_of(i)
        att = (mm(e_all[rows], vx[...]) / total_all[rows]).astype(BF16)
        att_all[rows] = att
        xp[core, 0, :hd, rows] = att.T
        dvt[...] += mm(dtr[:, rows], normed_all[rows].astype(BF16))
        return carry

    forward_cols(0)
    lax.fori_loop(0, n // 2, weigh, 0, unroll=2)
    each_peer(lambda src: heads_in(src, 1).wait_recv())
    for b in range(n):
        rows = slice(b * BLOCK, (b + 1) * BLOCK)
        vd = recv1[b, 1]
        vx[rows] = vd[:, :hd]
        vdt = vd.T
        vt[:, rows] = vdt[:hd]
        dtr[:, rows] = vdt[hd:]

    lax.fori_loop(0, n // 2, forward, 0, unroll=2)
    xp[core, 0, hd:] = dvt[...].astype(BF16)
    pair_out(0).start()

    for b in range(n):
        rows = slice(b * BLOCK, (b + 1) * BLOCK)
        bk[0, rows] = jnp.concatenate([att_all[rows], dvt[:, rows].T.astype(BF16)], axis=1)
    forward_cols(1)
    each_peer(lambda to: back_out(to, 0).start())

    def backward(i, carry):
        rows = pair_of(i)
        dab = two_blocks(i, 1)[:, hd:]
        delta = jnp.sum(dab.astype(F32) * att_all[rows].astype(F32), axis=1, keepdims=True)
        ds = (normed_all[rows] * (mm(dab, vt[...]) - delta)).astype(BF16)
        dkt[...] += mm(qtr[:, rows], ds)
        dq = (mm(ds, kx[...]) * scale).astype(BF16)
        dq_all[rows] = dq
        xp[core, 1, :hd, rows] = dq.T
        return carry

    def grads_out(i, k0, count, stage):
        chip_to = lax.rem(chip + i, chips)
        rep_to = lax.rem(rep + i // chips, reps)
        to = chip_to * reps + rep_to
        here = chip * reps + rep
        return remote(
            gs.at[to, pl.ds(k0, count)], gr.at[here, pl.ds(k0, count)],
            ssg.at[stage, to], rsg.at[stage, here], 2 * chip_to + core, rep_to,
        )

    def grads_in(i, k0, count, stage):
        chip_from = lax.rem(chip + i, chips)
        rep_from = lax.rem(rep + i // chips, reps)
        src = chip_from * reps + rep_from
        return remote(
            gs.at[src, pl.ds(k0, count)], gr.at[src, pl.ds(k0, count)],
            ssg.at[stage, src], rsg.at[stage, src], 2 * chip_from + core, rep_from,
        )

    stages = ((2, 1, 0), (3, 1, 1), (0, 2, 2))

    def each_group(act):
        def step(i, carry):
            act(i)
            return carry

        lax.fori_loop(1, chips * reps, step, 0)

    def product(kinds, column_kind, piece, rows):
        left = jnp.concatenate(
            [xp[c, piece][r] for r in rows for c in range(2)], axis=0
        )
        right = trecv[:, column_kind].reshape(n * BLOCK, trecv.shape[3])
        total = mm(left, right).astype(BF16)
        for j, kind in enumerate(kinds):
            one = total[2 * hd * j : 2 * hd * (j + 1)].T
            gs[:, kind] = one.reshape(chips * reps, part, 2 * hd)

    low, high = slice(0, hd), slice(hd, 2 * hd)
    lax.fori_loop(0, 2, backward, 0, unroll=2)
    finish_cols(0)
    pair_in(0).wait_recv()
    product((2,), 0, 0, (high,))
    each_group(lambda i: grads_out(i, *stages[0]).start())
    lax.fori_loop(2, n // 2, backward, 0, unroll=2)

    xp[core, 1, hd:] = dkt[...].astype(BF16)
    pair_out(1).start()
    finish_cols(1)
    product((3,), 1, 0, (low,))
    each_group(lambda i: grads_out(i, *stages[1]).start())
    pair_in(1).wait_recv()
    product((0, 1), 0, 1, (low, high))
    each_group(lambda i: grads_out(i, *stages[2]).start())
    gr[pl.ds(chip * reps + rep, 1)] = gs[pl.ds(chip * reps + rep, 1)]

    for b in range(n):
        rows = slice(b * BLOCK, (b + 1) * BLOCK)
        bk[1, rows] = jnp.concatenate([dq_all[rows], dkt[:, rows].T.astype(BF16)], axis=1)
    each_peer(lambda to: back_out(to, 1).start())
    mine = pl.ds(pl.multiple_of(me * BLOCK, BLOCK), BLOCK)
    for piece in range(2):
        back[me, piece] = bk[piece, mine]

    each_peer(lambda src: back_in(src, 0).wait_recv())
    att = jnp.concatenate([back[h, 0][:, :hd] for h in range(n)], axis=1)
    dv = jnp.concatenate([back[h, 0][:, hd:] for h in range(n)], axis=1)
    out[0] = mm_nt(att, w[3]).astype(BF16)
    each_peer(lambda src: back_in(src, 1).wait_recv())
    dq = jnp.concatenate([back[h, 1][:, :hd] for h in range(n)], axis=1)
    dk = jnp.concatenate([back[h, 1][:, hd:] for h in range(n)], axis=1)
    dinp[0] = (mm_nt(dq, w[0]) + mm_nt(dk, w[1]) + mm_nt(dv, w[2])).astype(BF16)

    def drain(to):
        for piece in range(2):
            heads_out(to, piece).wait_send()
            back_out(to, piece).wait_send()

    each_peer(drain)
    for kind in range(2):
        near(kind, lambda to, kind: cols_out(to, kind).wait_send())
        for k in range(2):
            cols_on(kind, k).wait_send()
    pair_out(0).wait_send()
    pair_out(1).wait_send()
    for stage in stages:
        each_group(lambda i, stage=stage: grads_out(i, *stage).wait_send())
        each_group(lambda i, stage=stage: grads_in(i, *stage).wait_recv())
        kinds = slice(stage[0], stage[0] + stage[1])
        for c in range(chips):
            acc = gr[c * reps, kinds].astype(F32)
            for r in range(1, reps):
                acc = acc + gr[c * reps + r, kinds].astype(F32)
            grads[kinds, :, c * 2 * hd : (c + 1) * 2 * hd] = acc


def by_heads(n, reps, tokens, cotangent, weights, neighbour_lists, neighbour_counts):
    width = tokens.shape[2]
    slab = n * BLOCK
    cols = weights.shape[2]
    part = width // (n * reps)
    groups = (n // 2) * reps
    vmem = pl.BlockSpec(memory_space=pltpu.VMEM)
    hbm = pl.BlockSpec(memory_space=pl.ANY)
    dma = pltpu.SemaphoreType.DMA
    return pl.pallas_call(
        functools.partial(layer_kernel, n, reps),
        out_shape=(
            jax.ShapeDtypeStruct(tokens.shape, BF16),
            jax.ShapeDtypeStruct(tokens.shape, BF16),
            jax.ShapeDtypeStruct((4, part, cols), F32),
        ),
        in_specs=[hbm] * 3 + [vmem] * 2,
        out_specs=(vmem, vmem, vmem),
        scratch_shapes=[
            pltpu.VMEM((BLOCK, width), BF16),
            pltpu.VMEM((BLOCK, width), BF16),
            pltpu.VMEM(weights.shape, BF16),
            pltpu.VMEM((n, 2, BLOCK, 2 * HEAD_DIM), BF16),
            pltpu.VMEM((n, 2, BLOCK, 2 * HEAD_DIM), BF16),
            pltpu.VMEM((2, 2, BLOCK, width // 2), BF16),
            pltpu.VMEM((n, 2, BLOCK, width // 2), BF16),
            pltpu.VMEM((HEAD_DIM, slab), BF16),
            pltpu.VMEM((HEAD_DIM, slab), BF16),
            pltpu.VMEM((HEAD_DIM, slab), BF16),
            pltpu.VMEM((HEAD_DIM, slab), BF16),
            pltpu.VMEM((slab, HEAD_DIM), BF16),
            pltpu.VMEM((slab, HEAD_DIM), BF16),
            pltpu.VMEM((HEAD_DIM, slab), F32),
            pltpu.VMEM((HEAD_DIM, slab), F32),
            pltpu.VMEM((n, slab), F32),
            pltpu.VMEM((slab, slab), F32),
            pltpu.VMEM((slab, slab), BF16),
            pltpu.VMEM((slab, 1), F32),
            pltpu.VMEM((slab, HEAD_DIM), BF16),
            pltpu.VMEM((slab, HEAD_DIM), BF16),
            pltpu.VMEM((2, 2, 2 * HEAD_DIM, slab), BF16),
            pltpu.VMEM((2, slab, 2 * HEAD_DIM), BF16),
            pltpu.VMEM((n, 2, BLOCK, 2 * HEAD_DIM), BF16),
            pltpu.VMEM((groups, 4, part, 2 * HEAD_DIM), BF16),
            pltpu.VMEM((groups, 4, part, 2 * HEAD_DIM), BF16),
            dma((6,)),
            dma((2, n)), dma((2, n)), dma((2, n)), dma((2, n)), dma((2, 2)),
            dma((2, n)), dma((2, n)),
            dma((2,)), dma((2,)), dma((3, groups)), dma((3, groups)),
        ],
        compiler_params=pltpu.CompilerParams(
            collective_id=0, has_side_effects=True, vmem_limit_bytes=53 * 1024 * 1024
        ),
        cost_estimate=pl.CostEstimate(
            flops=3 * 10**9, bytes_accessed=6 * 2**20, transcendentals=2**20
        ),
    )(tokens, cotangent, weights, neighbour_lists, neighbour_counts)


def split_heads(matrix):
    return matrix.reshape(matrix.shape[:-1] + (HEADS, HEAD_DIM))


def body(tokens, cotangent, weights, neighbour_lists, neighbour_counts):
    score_scale = 1.0 / math.sqrt(HEAD_DIM)
    inputs = tokens[0]
    upstream = cotangent[0]
    row_count = inputs.shape[0]
    local_blocks = row_count // BLOCK
    w_query, w_key, w_value, w_out = (weights[0], weights[1], weights[2], weights[3])
    queries = (
        jnp.dot(inputs, w_query, preferred_element_type=jnp.float32)
        .astype(jnp.bfloat16)
        .reshape(local_blocks, BLOCK, -1)
    )
    key_rows = (
        jnp.dot(inputs, w_key, preferred_element_type=jnp.float32)
        .astype(jnp.bfloat16)
        .reshape(local_blocks, BLOCK, -1)
    )
    value_rows = (
        jnp.dot(inputs, w_value, preferred_element_type=jnp.float32)
        .astype(jnp.bfloat16)
        .reshape(local_blocks, BLOCK, -1)
    )
    all_keys, all_values = (
        lax.all_gather(key_rows, "seq", axis=0, tiled=True),
        lax.all_gather(value_rows, "seq", axis=0, tiled=True),
    )
    slab_blocks = all_keys.shape[0]
    first_block = lax.axis_index("seq") * local_blocks
    lists_all = neighbour_lists[0]
    counts_all = neighbour_counts[0]
    my_lists = lax.dynamic_slice_in_dim(lists_all, first_block, local_blocks, 0)
    my_counts = lax.dynamic_slice_in_dim(counts_all, first_block, local_blocks, 0)
    slot_keys = split_heads(
        jnp.take(all_keys, my_lists, axis=0).reshape(local_blocks, MAXN * BLOCK, -1)
    )
    slot_values = split_heads(
        jnp.take(all_values, my_lists, axis=0).reshape(local_blocks, MAXN * BLOCK, -1)
    )
    query_heads = split_heads(queries)
    scores = (
        jnp.einsum("bqhd,bkhd->bhqk", query_heads, slot_keys, preferred_element_type=jnp.float32)
        * score_scale
    )
    live_cols = (jnp.arange(MAXN * BLOCK) // BLOCK)[None, :] < my_counts[:, None]
    scores = jnp.where(live_cols[:, None, None, :], scores, -1e30)
    row_max = jnp.max(scores, axis=-1)
    exponent = jnp.exp(scores - row_max[..., None])
    totals = jnp.sum(exponent, axis=-1)
    mixed = jnp.einsum(
        "bhqk,bkhd->bqhd",
        exponent.astype(jnp.bfloat16),
        slot_values,
        preferred_element_type=jnp.float32,
    )
    attended = (
        (mixed / jnp.transpose(totals, (0, 2, 1))[..., None])
        .astype(jnp.bfloat16)
        .reshape(row_count, -1)
    )
    output = lax.dot_general(
        attended, w_out, (((1,), (1,)), ((), ())), preferred_element_type=jnp.float32
    ).astype(jnp.bfloat16)
    d_attended = jnp.dot(upstream, w_out, preferred_element_type=jnp.float32).astype(jnp.bfloat16)
    grad_out = lax.dot_general(
        upstream, attended, (((0,), (0,)), ((), ())), preferred_element_type=jnp.float32
    )
    d_blocks = d_attended.reshape(local_blocks, BLOCK, -1)
    d_heads = split_heads(d_blocks)
    attended_heads = split_heads(attended.reshape(local_blocks, BLOCK, -1))
    row_delta = jnp.transpose(
        jnp.sum(d_heads.astype(jnp.float32) * attended_heads.astype(jnp.float32), axis=-1),
        (0, 2, 1),
    )
    normed = exponent / totals[..., None]
    d_probs = jnp.einsum(
        "bqhd,bkhd->bhqk", d_heads, slot_values, preferred_element_type=jnp.float32
    )
    d_scores = (normed * (d_probs - row_delta[..., None])).astype(jnp.bfloat16)
    d_queries = (
        (
            jnp.einsum("bhqk,bkhd->bqhd", d_scores, slot_keys, preferred_element_type=jnp.float32)
            * score_scale
        )
        .astype(jnp.bfloat16)
        .reshape(row_count, -1)
    )
    gathered_query, gathered_dattn = (
        lax.all_gather(queries, "seq", axis=0, tiled=True),
        lax.all_gather(d_blocks, "seq", axis=0, tiled=True),
    )
    gathered_max, gathered_total, gathered_delta = (
        lax.all_gather(row_max, "seq", axis=0, tiled=True),
        lax.all_gather(totals, "seq", axis=0, tiled=True),
        lax.all_gather(row_delta, "seq", axis=0, tiled=True),
    )
    owners = first_block + jnp.arange(local_blocks)
    live_slots = jnp.arange(MAXN)[None, :] < counts_all[:, None]
    listed = jnp.any(
        (lists_all[:, :, None] == owners[None, None, :]) & live_slots[:, :, None], axis=1
    )
    groups = slab_blocks // 8
    own_keys = split_heads(key_rows)
    own_values = split_heads(value_rows)

    def regroup(matrix):
        return matrix.reshape((groups, 8) + matrix.shape[1:])

    def accumulate(carry, group_data):
        group_query, group_dattn, group_max, group_total, group_delta, group_listed = group_data
        group_query = split_heads(group_query)
        group_dattn = split_heads(group_dattn)
        group_scores = (
            jnp.einsum(
                "cqhd,ikhd->cihqk", group_query, own_keys, preferred_element_type=jnp.float32
            )
            * score_scale
        )
        group_scores = jnp.where(group_listed[:, :, None, None, None], group_scores, -1e30)
        group_probs = (
            jnp.exp(group_scores - group_max[:, None, :, :, None])
            / group_total[:, None, :, :, None]
        )
        group_dprobs = jnp.einsum(
            "cqhd,ikhd->cihqk", group_dattn, own_values, preferred_element_type=jnp.float32
        )
        group_dscores = (group_probs * (group_dprobs - group_delta[:, None, :, :, None])).astype(
            jnp.bfloat16
        )
        key_next = carry[0] + jnp.einsum(
            "cihqk,cqhd->ikhd", group_dscores, group_query, preferred_element_type=jnp.float32
        )
        value_next = carry[1] + jnp.einsum(
            "cihqk,cqhd->ikhd",
            group_probs.astype(jnp.bfloat16),
            group_dattn,
            preferred_element_type=jnp.float32,
        )
        return ((key_next, value_next), None)

    zero_sum = jnp.zeros((local_blocks, BLOCK, HEADS, HEAD_DIM), jnp.float32)
    group_inputs = (
        regroup(gathered_query),
        regroup(gathered_dattn),
        regroup(gathered_max),
        regroup(gathered_total),
        regroup(gathered_delta),
        regroup(listed),
    )
    (key_heads, value_heads), _ = lax.scan(accumulate, (zero_sum, zero_sum), group_inputs)
    key_sum = (key_heads * score_scale).reshape(local_blocks, BLOCK, -1)
    value_sum = value_heads.reshape(local_blocks, BLOCK, -1)
    d_keys = key_sum.astype(jnp.bfloat16).reshape(row_count, -1)
    d_values = value_sum.astype(jnp.bfloat16).reshape(row_count, -1)
    stacked = jnp.concatenate([d_queries, d_keys, d_values], axis=1)
    w_joined = jnp.concatenate([w_query, w_key, w_value], axis=1)
    d_inputs = lax.dot_general(
        stacked, w_joined, (((1,), (1,)), ((), ())), preferred_element_type=jnp.float32
    ).astype(jnp.bfloat16)
    grad_joined = lax.dot_general(
        inputs, stacked, (((0,), (0,)), ((), ())), preferred_element_type=jnp.float32
    )
    width_model = inputs.shape[1]
    grad_three = jnp.transpose(grad_joined.reshape(width_model, 3, -1), (1, 0, 2))
    grads = jnp.concatenate([grad_three, grad_out[None]], axis=0)
    within_slab = lax.psum_scatter(
        grads.astype(jnp.bfloat16), "seq", scatter_dimension=1, tiled=True
    )
    summed = lax.psum_scatter(within_slab, "rep", scatter_dimension=1, tiled=True).astype(
        jnp.float32
    )
    return (output[None], d_inputs[None], summed)


def solution(mesh):
    placed = (
        P("rep", "seq", None),
        P("rep", "seq", None),
        P(),
        P("rep", None, None),
        P("rep", None),
    )
    n, reps = mesh.shape["seq"], mesh.shape["rep"]
    run = functools.partial(by_heads, n, reps) if n == HEADS else body
    return jax.shard_map(
        run,
        mesh=mesh,
        in_specs=placed,
        out_specs=(P("rep", "seq", None), P("rep", "seq", None), P(None, ("seq", "rep"), None)),
        check_vma=False,
    )
```
